128 devices in a mesh: dp: 32 (over x, z_hi, y), band: 4 (over z_lo, core).
Axes of the slice: x: 4, y: 4, z: 4 (z_hi: 2, z_lo: 2; z = z_hi * 2 + z_lo), core: 2. Of those that a mesh axis runs over, the one named last changes fastest.
Arguments:
- tokens: bfloat16 [32, 1536, 768], P('dp', 'band'), may hold values from -6 to 6
- lengths: int32 [32, 8], P('dp'), may hold values from 1 to 1153, 1536 in all within a row
- ln1_gain: float32 [768], replicated, may hold values from 0.25 to 1.75
- ln1_bias: float32 [768], replicated, may hold values from -1.75 to 1.75
- w_query: bfloat16 [768, 768], replicated, may hold values from -0.21875 to 0.21875
- b_query: float32 [768], replicated, may hold values from -1.75 to 1.75
- w_key: bfloat16 [768, 768], replicated, may hold values from -0.21875 to 0.21875
- w_value: bfloat16 [768, 768], replicated, may hold values from -0.21875 to 0.21875
- b_value: float32 [768], replicated, may hold values from -1.75 to 1.75
- w_out: bfloat16 [768, 768], replicated, may hold values from -1.75 to 1.75
- b_out: float32 [768], replicated, may hold values from -1.75 to 1.75
- ln2_gain: float32 [768], replicated, may hold values from 0.25 to 1.75
- ln2_bias: float32 [768], replicated, may hold values from -1.75 to 1.75
- w_up: bfloat16 [768, 3072], replicated, may hold values from -0.21875 to 0.21875
- b_up: float32 [3072], replicated, may hold values from -1.75 to 1.75
- w_down: bfloat16 [3072, 768], replicated, may hold values from -0.109375 to 0.109375
- b_down: float32 [768], replicated, may hold values from -1.75 to 1.75
- cotangent: bfloat16 [32, 1536, 768], P('dp', 'band'), may hold values from -6 to 6
Outputs:
- layer_out: bfloat16 [32, 1536, 768], P('dp', 'band')
- grad_tokens: float32 [32, 1536, 768], P('dp', 'band')
- grad_ln1_gain: float32 [768], replicated
- grad_ln1_bias: float32 [768], replicated
- grad_w_query: float32 [768, 768], replicated
- grad_b_query: float32 [768], replicated
- grad_w_key: float32 [768, 768], replicated
- grad_w_value: float32 [768, 768], replicated
- grad_b_value: float32 [768], replicated
- grad_w_out: float32 [768, 768], replicated
- grad_b_out: float32 [768], replicated
- grad_ln2_gain: float32 [768], replicated
- grad_ln2_bias: float32 [768], replicated
- grad_w_up: float32 [768, 3072], replicated
- grad_b_up: float32 [3072], replicated
- grad_w_down: float32 [3072, 768], replicated
- grad_b_down: float32 [768], replicated
The draws below stay inside these ranges and needn't reach their ends.
Inputs may be any that keep to these rules, and one draw needn't show every extreme that they name: `lengths`: each row sums to 1536; the largest tile of every sequence has exactly 1153 tokens.
All inputs are finite; a program needn't handle non-finite values.
Results may differ from the reference program's by a relative error of at most 0.012.
Values may be sent and summed in bfloat16 or wider, within the bound.
No kernel may reach another device: no remote copies, remote signals or barrier semaphores. Data moves between devices by JAX's collectives and lax.ppermute only.
A program may use at most 256 MiB of HBM per device.

```python
import math
import jax
import jax.numpy as jnp
import numpy as np
from jax import lax

D = 768
FF = 3072
HEADS = 12
HDIM = 64
LEN = 1536
TILES = 8
NSEQ = 32
SLICE = 384


def shard_levels(rng, dims, shards, smallest, top_value):
    def one(dim, shards_of):
        draws = jax.random.uniform(jax.random.fold_in(jax.random.fold_in(rng, 6), dim), (shards_of,), jnp.float32, smallest / len(shards), top_value / len(shards))
        return jnp.repeat(jnp.exp(draws), dims[dim] // shards_of).reshape((-1,) + (1,) * (len(dims) - dim - 1))

    gain = one(*shards[0])
    for cut in shards[1:]:
        gain = gain * one(*cut)
    return gain


def length_profile(number_of, total, limit, slope):
    loads = [(1 << 20) // math.isqrt(standing ** slope) + 1 for standing in range(2, number_of + 1)]
    spare, holding = total - limit - (number_of - 1), [1] * (number_of - 1)
    while spare > 0:
        free = [i for i in range(number_of - 1) if holding[i] < limit]
        whole, budget = sum([loads[i] for i in free]), spare
        for i in free:
            extra = min(limit - holding[i], max(1, budget * loads[i] // whole), spare)
            holding[i] = holding[i] + extra
            spare = spare - extra
    return np.array([limit] + holding)


def ragged_sizes(own_key, amount, total, reach, lean):
    if amount == 2:
        one = jax.random.randint(own_key, (), max(1, total - reach), min(reach, total - 1) + 1)
        return jnp.stack([one, total - one])
    tallies = jnp.asarray(length_profile(amount, total, reach, lean), jnp.int32)
    pairs = (amount - 1) // 2
    giver, taker = tallies[1:1 + 2 * pairs:2], tallies[2:2 + 2 * pairs:2]
    slack = jnp.minimum(giver - 1, reach - taker)
    shifted = jax.random.randint(jax.random.fold_in(own_key, 1), (pairs,), 0, 1 << 20) % (slack + 1)
    tallies = tallies.at[1:1 + 2 * pairs:2].set(giver - shifted).at[2:2 + 2 * pairs:2].set(taker + shifted)
    return tallies[jax.random.permutation(jax.random.fold_in(own_key, 2), amount)]


def bell_draw(stream_key, extent, deviation, limit, split=(), kind=jnp.bfloat16):
    gain = shard_levels(stream_key, extent, split, -0.22, 0.18) if split else 1.0
    result = jax.random.normal(stream_key, extent, jnp.float32) * deviation * gain
    return jnp.minimum(jnp.maximum(result, -limit), limit).astype(kind)


def setup_inputs(seed: int = 0) -> dict:
    streams_of = jax.random.split(jax.random.key(seed), 19)
    return {
        "tokens": bell_draw(streams_of[0], (NSEQ, LEN, D), 1.0, 6.0, ((0, 32), (1, 4))),
        "lengths": jax.vmap(lambda own: ragged_sizes(own, TILES, LEN, 3 * SLICE + 1, 2))(jax.random.split(streams_of[1], NSEQ)).reshape((NSEQ, TILES)).astype(jnp.int32),
        "ln1_gain": jnp.clip(1.0 + 0.15 * jax.random.normal(streams_of[2], (D,), jnp.float32), 0.25, 1.75),
        "ln1_bias": bell_draw(streams_of[3], (D,), 0.3, 1.75, (), jnp.float32),
        "w_query": bell_draw(streams_of[4], (D, D), D ** -0.5, 0.21875),
        "b_query": bell_draw(streams_of[5], (D,), 0.3, 1.75, (), jnp.float32),
        "w_key": bell_draw(streams_of[6], (D, D), D ** -0.5, 0.21875),
        "w_value": bell_draw(streams_of[7], (D, D), D ** -0.5, 0.21875),
        "b_value": bell_draw(streams_of[8], (D,), 0.3, 1.75, (), jnp.float32),
        "w_out": bell_draw(streams_of[9], (D, D), (D // 64) ** -0.5, 1.75),
        "b_out": bell_draw(streams_of[10], (D,), 0.3, 1.75, (), jnp.float32),
        "ln2_gain": jnp.clip(1.0 + 0.15 * jax.random.normal(streams_of[11], (D,), jnp.float32), 0.25, 1.75),
        "ln2_bias": bell_draw(streams_of[12], (D,), 0.3, 1.75, (), jnp.float32),
        "w_up": bell_draw(streams_of[13], (D, FF), D ** -0.5, 0.21875),
        "b_up": bell_draw(streams_of[14], (FF,), 0.3, 1.75, (), jnp.float32),
        "w_down": bell_draw(streams_of[15], (FF, D), FF ** -0.5, 0.109375),
        "b_down": bell_draw(streams_of[16], (D,), 0.3, 1.75, (), jnp.float32),
        "cotangent": bell_draw(streams_of[17], (NSEQ, LEN, D), 1.0, 6.0, ((0, 32), (1, 4))),
    }


@jax.custom_vjp
def low(v):
    return lax.optimization_barrier(v.astype(jnp.bfloat16)).astype(jnp.float32)

@jax.custom_vjp
def low_back(v):
    return v

def low_keep(v):
    return (low(v), None)

def low_pass(kept, grad):
    return (grad,)

def back_keep(v):
    return (v, None)

def back_low(kept, grad):
    return (low(grad),)
low.defvjp(low_keep, low_pass)
low_back.defvjp(back_keep, back_low)

def matmul(left, right):
    return jnp.dot(left, right, precision=lax.Precision.HIGHEST)

def normalize(values):
    centre = values - lax.optimization_barrier(jnp.mean(values, axis=-1, keepdims=True))
    return centre * lax.rsqrt(lax.optimization_barrier(jnp.mean(centre * centre, axis=-1, keepdims=True)) + 1e-06)

def forward(inputs, seg_ids, params):
    ln1_gain, ln1_bias, w_query, b_query, w_key, w_value, b_value, w_out, b_out, ln2_gain, ln2_bias, w_up, b_up, w_down, b_down = params
    attn_in = low(normalize(inputs) * ln1_gain + ln1_bias)
    query = low_back(low(matmul(attn_in, w_query) + b_query))
    key_rows = low_back(low(matmul(attn_in, w_key)))
    value_rows = low_back(low(matmul(attn_in, w_value) + b_value))
    query_h = query.reshape(LEN, HEADS, HDIM)
    key_h = key_rows.reshape(LEN, HEADS, HDIM)
    value_h = value_rows.reshape(LEN, HEADS, HDIM)
    scores = jnp.einsum('qhd,khd->hqk', query_h, key_h, precision=lax.Precision.HIGHEST) * 0.125
    scores = low_back(scores)
    allowed = seg_ids[:, None] == seg_ids[None, :]
    scores = jnp.where(allowed[None], scores, -1e+30)
    weights = low(jax.nn.softmax(scores, axis=-1))
    mixed = jnp.einsum('hqk,khd->qhd', weights, value_h, precision=lax.Precision.HIGHEST)
    mixed = low_back(low(mixed.reshape(LEN, D)))
    attn_branch = low_back(matmul(mixed, w_out) + b_out)
    hidden1 = inputs + attn_branch
    mlp_in = low(normalize(hidden1) * ln2_gain + ln2_bias)
    pre_act = low_back(matmul(mlp_in, w_up) + b_up)
    activ = low(jax.nn.gelu(pre_act, approximate=False))
    mlp_branch = low_back(matmul(activ, w_down) + b_down)
    return hidden1 + mlp_branch

def reference(tokens, lengths, ln1_gain, ln1_bias, w_query, b_query, w_key, w_value, b_value, w_out, b_out, ln2_gain, ln2_bias, w_up, b_up, w_down, b_down, cotangent):
    params = tuple((p.astype(jnp.float32) for p in (ln1_gain, ln1_bias, w_query, b_query, w_key, w_value, b_value, w_out, b_out, ln2_gain, ln2_bias, w_up, b_up, w_down, b_down)))
    ends = jnp.cumsum(lengths, axis=1)
    places = jnp.arange(LEN, dtype=jnp.int32)
    seg_all = lax.optimization_barrier(jnp.sum((places[None, :, None] >= ends[:, None, :]).astype(jnp.int32), axis=2))
    inputs_all = tokens.astype(jnp.float32)
    upstream_all = cotangent.astype(jnp.float32)

    def one_sequence(carry, items):
        inputs, seg_ids, upstream = items
        outputs, pull = jax.vjp(lambda xin, pin: forward(xin, seg_ids, pin), inputs, params)
        grad_in, grad_params = pull(upstream)
        carry = jax.tree.map(lambda acc, new: acc + new, carry, grad_params)
        return (carry, (outputs.astype(jnp.bfloat16), grad_in))
    start = jax.tree.map(jnp.zeros_like, params)
    totals, (layer_out, grad_tokens) = lax.scan(one_sequence, start, (inputs_all, seg_all, upstream_all))
    return (layer_out, grad_tokens) + tuple(totals)
```

```python
import jax
import jax.numpy as jnp
from jax import lax
from jax.experimental import pallas as pl
from jax.experimental.pallas import tpu as pltpu
from jax.sharding import PartitionSpec as P

HEADS = 12
HDIM = 64
PAIR = 2 * HDIM
SEGS = 128
BARRED = 2.0**100
BF = jnp.bfloat16
F32 = jnp.float32
BOTH = ("dp", "band")
CORE = [(0, 1), (1, 0), (2, 3), (3, 2)]
ZLO = [(0, 2), (1, 3), (2, 0), (3, 1)]
BIT_A = (0, 1, 1, 0)
BIT_B = (0, 0, 1, 1)
PARAMS = pltpu.CompilerParams(vmem_limit_bytes=56 * 2**20)


def place_of(device):
    dp, band = divmod(device, 4)
    x, rest = divmod(dp, 8)
    z_hi, y = divmod(rest, 4)
    z_lo, core = divmod(band, 2)
    return x, y, z_hi * 2 + z_lo, core


def cube_groups(first):
    groups = {}
    for device in range(128):
        x, y, z, core = place_of(device)
        fixed, moving = (BIT_B, BIT_A) if (core == 0) == first else (BIT_A, BIT_B)
        members = groups.setdefault((core, fixed[x], fixed[y], fixed[z]), [])
        members.append(((moving[x], moving[y], moving[z]), device))
    return [[device for _, device in sorted(members)] for members in groups.values()]


GROUPS_1 = cube_groups(True)
GROUPS_2 = cube_groups(False)
GROUPS_ALL = [[d for d in range(128) if d % 2 == core] for core in range(2)]


def matmul(left, right):
    return jnp.dot(left, right, preferred_element_type=F32)


def trans_left(left, right):
    return lax.dot_general(left, right, (((0,), (0,)), ((), ())), preferred_element_type=F32)


def trans_right(left, right):
    return lax.dot_general(left, right, (((1,), (1,)), ((), ())), preferred_element_type=F32)


def swap_core(values):
    return lax.ppermute(values, "band", CORE)


def swap_z(values):
    return lax.ppermute(values, "band", ZLO)


def norm_forward(values):
    centre = values - jnp.mean(values, axis=-1, keepdims=True)
    rscale = lax.rsqrt(jnp.mean(centre * centre, axis=-1, keepdims=True) + 1e-06)
    return centre * rscale, rscale


def norm_back(grad_norm, normed, rscale):
    first = jnp.mean(grad_norm, axis=-1, keepdims=True)
    second = jnp.mean(grad_norm * normed, axis=-1, keepdims=True)
    return rscale * (grad_norm - first - normed * second)


def column_sum(values):
    return jnp.sum(values, axis=0, keepdims=True)


def shape(values, dtype, *dims):
    return jax.ShapeDtypeStruct(dims, dtype)


def whole(*dims):
    return pl.BlockSpec(dims, lambda i, core: (0,) * len(dims))


def by_core(dims, axis):
    return pl.BlockSpec(dims, lambda i, core: tuple(core[0] if k == axis else 0 for k in range(len(dims))))


def call(kernel, name, core, ins, in_specs, outs, scratch=(), flops=0):
    traffic = sum(x.size * x.dtype.itemsize for x in list(ins) + list(outs))
    return pl.pallas_call(
        kernel,
        grid_spec=pltpu.PrefetchScalarGridSpec(
            num_scalar_prefetch=1,
            grid=(1,),
            in_specs=in_specs,
            out_specs=[whole(*x.shape) for x in outs],
            scratch_shapes=list(scratch),
        ),
        out_shape=list(outs),
        compiler_params=PARAMS,
        cost_estimate=pl.CostEstimate(flops=flops, bytes_accessed=traffic, transcendentals=0),
        name=name,
    )(core, *ins)


def project_kernel(core, x0, x1, gain, bias, wq, bq, wk, wv, bv, a_ref, k_ref, v_ref, q_ref=None):
    inputs = jnp.concatenate([x0[...], x1[...]], axis=0).astype(F32)
    normed, _ = norm_forward(inputs)
    attn_in = (normed * gain[...] + bias[...]).astype(BF)
    a_ref[...] = attn_in
    if q_ref is not None:
        q_ref[...] = (matmul(attn_in, wq[...]) + bq[...]).astype(BF) * 0.125
    k_ref[...] = matmul(attn_in, wk[...]).astype(BF)
    v_ref[...] = (matmul(attn_in, wv[...]) + bv[...]).astype(BF)


def project(core, x0, x1, gain, bias, wq, bq, wk, wv, bv, with_query):
    rows, width = x0.shape
    half = width // 2
    outs = [jax.ShapeDtypeStruct((2 * rows, width), BF)] + [
        jax.ShapeDtypeStruct((2 * rows, half), BF)
    ] * (3 if with_query else 2)
    weight, vector = by_core((width, half), 1), by_core((1, half), 1)
    return call(
        project_kernel,
        "project",
        core,
        (x0, x1, gain, bias, wq, bq, wk, wv, bv),
        [whole(rows, width)] * 2 + [whole(1, width)] * 2 + [weight, vector, weight, weight, vector],
        outs,
        flops=2 * 2 * rows * width * half * (len(outs) - 1),
    )


def head_rows(head, dims):
    return lax.broadcasted_iota(jnp.int32, dims, 0) // HDIM == head


def head_lanes(head, dims):
    return lax.broadcasted_iota(jnp.int32, dims, 1) // HDIM == head


KEY_BLOCK = 256
MAX_ROWS = 32


def attend_kernel(core, q_ref, k0, k1, v0, v1, mq_ref, mk_ref, o_ref, lse_ref, s_buf, p_buf, rhs, vt, kx):
    nq, width = q_ref.shape
    near = k0.shape[0]
    nk = 2 * near
    heads = width // HDIM
    blocks = nk // KEY_BLOCK

    def prepare(head):
        pair = slice((head // 2) * PAIR, (head // 2 + 1) * PAIR)
        if head % 2 == 0:
            vt[(head // 2) % 2, :PAIR, :near] = v0[:, pair].T
            vt[(head // 2) % 2, :PAIR, near:] = v1[:, pair].T
            kx[(head // 2) % 2, :near, :PAIR] = k0[:, pair]
            kx[(head // 2) % 2, near:, :PAIR] = k1[:, pair]
        turned = q_ref[:, pair].T
        rhs[head % 2, :PAIR] = jnp.where(
            head_rows(head % 2, turned.shape), turned, jnp.zeros((), BF)
        )

    for i in range(2):
        vt[i, PAIR:] = jnp.ones((16, nk), BF)
        rhs[i, PAIR:] = mq_ref[...]
        kx[i, :, PAIR:] = mk_ref[...]
    peaks, outs, logs = {}, [], []
    for t in range(heads + 2):
        if t < heads:
            prepare(t)
        peak, total = None, None
        for i in range(blocks):
            rows = slice(i * KEY_BLOCK, (i + 1) * KEY_BLOCK)
            if t < heads:
                scores = matmul(kx[(t // 2) % 2, rows, :], rhs[t % 2])
                s_buf[t % 2, rows, :] = scores
                for j in range(KEY_BLOCK // MAX_ROWS):
                    part = scores[j * MAX_ROWS : (j + 1) * MAX_ROWS]
                    peak = part if peak is None else jnp.maximum(peak, part)
            if 0 <= t - 1 < heads:
                p_buf[(t - 1) % 2, rows, :] = jnp.exp(
                    s_buf[(t - 1) % 2, rows, :] - peaks[t - 1]
                ).astype(BF)
            if 0 <= t - 2 < heads:
                part = matmul(vt[((t - 2) // 2) % 2, :, rows], p_buf[(t - 2) % 2, rows, :])
                total = part if total is None else total + part
        if t < heads:
            peaks[t] = jnp.max(peak, axis=0, keepdims=True)
        if 0 <= t - 2 < heads:
            head = t - 2
            side = head % 2
            norm = total[PAIR : PAIR + 1]
            outs.append(total[side * HDIM : (side + 1) * HDIM] / norm)
            logs.append(peaks[head] + jnp.log(norm))
            if side == 1:
                pair = slice((head // 2) * PAIR, (head // 2 + 1) * PAIR)
                o_ref[:, pair] = jnp.concatenate(outs[-2:], axis=0).T.astype(BF)
    lse_ref[...] = jnp.concatenate(logs + [jnp.zeros((8 - heads, nq), F32)], axis=0)


def attend(core, query, key_near, key_far, value_near, value_far, mask_q, mask_k):
    nq, width = query.shape
    near = key_near.shape[0]
    nk = 2 * near
    return call(
        attend_kernel,
        "attend",
        core,
        (query, key_near, key_far, value_near, value_far, mask_q, mask_k),
        [whole(nq, width)] + [whole(near, width)] * 4 + [whole(SEGS, nq), whole(nk, SEGS)],
        [jax.ShapeDtypeStruct((nq, width), BF), jax.ShapeDtypeStruct((8, nq), F32)],
        [
            pltpu.VMEM((2, nk, nq), F32),
            pltpu.VMEM((2, nk, nq), BF),
            pltpu.VMEM((2, PAIR + SEGS, nq), BF),
            pltpu.VMEM((2, PAIR + 16, nk), BF),
            pltpu.VMEM((2, nk, PAIR + SEGS), BF),
        ],
        flops=2 * 2 * nq * nk * width * 4,
    )


QUERY_BLOCK = 256


def attend_back_kernel(
    core, q_ref, k0, k1, v0, v1, mq_ref, mk_ref, o_ref, g_ref, lse_ref, dq_ref, dk_ref, dv_ref, p_buf, ds_buf
):
    nq = q_ref.shape[0]
    nk = 2 * k0.shape[0]
    blocks = nq // QUERY_BLOCK
    nothing = jnp.zeros((), BF)
    query, grad = q_ref[...], g_ref[...]
    query_t, grad_t = query.T, grad.T
    key = jnp.concatenate([k0[...], k1[...]], axis=0)
    value = jnp.concatenate([v0[...], v1[...]], axis=0)
    key_t = key.T
    product = grad_t.astype(F32) * o_ref[...].T.astype(F32)
    key_masked = jnp.concatenate([key, mk_ref[...]], axis=1)
    mask_q = mq_ref[...]
    for b in range(blocks):
        cols = slice(b * QUERY_BLOCK, (b + 1) * QUERY_BLOCK)
        dqs = []
        for e in range(2):
            at = (e * blocks + b) * QUERY_BLOCK
            rows = head_rows(e, (PAIR, QUERY_BLOCK))
            query_e = jnp.where(rows, query_t[:, cols], nothing)
            grad_e = jnp.where(rows, grad_t[:, cols], nothing)
            scores = matmul(key_masked, jnp.concatenate([query_e, mask_q[:, cols]], axis=0))
            probs = jnp.exp(scores - lse_ref[0, e : e + 1, cols])
            p_buf[:, at : at + QUERY_BLOCK] = probs.astype(BF)
            grad_probs = matmul(value, grad_e)
            inner = jnp.sum(product[e * HDIM : (e + 1) * HDIM, cols], axis=0, keepdims=True)
            grad_scores = (probs * (grad_probs - inner)).astype(BF)
            ds_buf[:, at : at + QUERY_BLOCK] = grad_scores
            dqs.append(matmul(key_t, grad_scores)[e * HDIM : (e + 1) * HDIM])
        dq_ref[cols, :] = (jnp.concatenate(dqs, axis=0) * 0.125).T.astype(BF)

    def by_head(values):
        return jnp.concatenate(
            [jnp.where(head_lanes(e, values.shape), values, nothing) for e in range(2)], axis=0
        )

    dv_ref[...] = matmul(p_buf[...], by_head(grad)).astype(BF)
    dk_ref[...] = matmul(ds_buf[...], by_head(query)).astype(BF)


def attend_back(core, query, key_near, key_far, value_near, value_far, mask_q, mask_k, mixed, grad, lse):
    nq, width = query.shape
    near = key_near.shape[0]
    nk = 2 * near
    lse = lse[: 2 * (width // PAIR)].reshape(width // PAIR, 2, nq)
    pair = lambda rows: pl.BlockSpec((rows, PAIR), lambda i, core: (0, i))
    outs = [jax.ShapeDtypeStruct((rows, width), BF) for rows in (nq, nk, nk)]
    ins = (query, key_near, key_far, value_near, value_far, mask_q, mask_k, mixed, grad, lse)
    return pl.pallas_call(
        attend_back_kernel,
        grid_spec=pltpu.PrefetchScalarGridSpec(
            num_scalar_prefetch=1,
            grid=(width // PAIR,),
            in_specs=[pair(nq)]
            + [pair(near)] * 4
            + [whole(SEGS, nq), whole(nk, SEGS)]
            + [pair(nq)] * 2
            + [pl.BlockSpec((1, 2, nq), lambda i, core: (i, 0, 0))],
            out_specs=[pair(nq), pair(nk), pair(nk)],
            scratch_shapes=[pltpu.VMEM((nk, 2 * nq), BF)] * 2,
        ),
        out_shape=outs,
        compiler_params=PARAMS,
        cost_estimate=pl.CostEstimate(
            flops=2 * 5 * nq * nk * width * 4,
            bytes_accessed=sum(x.size * x.dtype.itemsize for x in ins + tuple(outs)),
            transcendentals=0,
        ),
        name="attend_back",
    )(core, *ins)


def middle_kernel(core, x_ref, mine, other, w_out, b_out, gain, bias, h_ref, c_ref):
    half = mine.shape[1]
    at = pl.multiple_of(core[0] * half, 128)
    away = pl.multiple_of((1 - core[0]) * half, 128)
    hidden1 = x_ref[...].astype(F32) + (
        matmul(mine[...], w_out[pl.ds(at, half), :])
        + matmul(other[...], w_out[pl.ds(away, half), :])
        + b_out[...]
    )
    h_ref[...] = hidden1
    normed, _ = norm_forward(hidden1)
    c_ref[...] = (normed * gain[...] + bias[...]).astype(BF)


def middle(core, x, mine, other, w_out, b_out, gain, bias):
    rows, width = x.shape
    half = width // 2
    return call(
        middle_kernel,
        "middle",
        core,
        (x, mine, other, w_out, b_out, gain, bias),
        [whole(rows, width), whole(rows, half), whole(rows, half), whole(width, width)]
        + [whole(1, width)] * 3,
        [jax.ShapeDtypeStruct((rows, width), F32), jax.ShapeDtypeStruct((rows, width), BF)],
        flops=2 * rows * width * width,
    )


HIDDEN_BLOCK = 512


def gelu_parts(values):
    bell = jnp.exp(values * values * -0.5)
    k = 1.0 / (1.0 + 0.23164188838 * jnp.abs(values))
    tail = 0.7107068705 + k * (-0.7265760135 + k * 0.5307027145)
    tail = k * (0.127414796 + k * (-0.142248368 + k * tail)) * bell
    below = jnp.where(values >= 0, 1.0 - tail, tail)
    return values * below, below + values * bell * 0.3989422804014327


def feed_kernel(
    core, c0, c1, g0, g1, w_up, b_up, w_down, dw_up, dw_down, db_up, out0, out1, dc0, dc1, pre, dact, act, gpre
):
    rows = c0.shape[0]
    normed = jnp.concatenate([c0[...], c1[...]], axis=0)
    grad = jnp.concatenate([g0[...], g1[...]], axis=0)
    steps = w_up.shape[1] // HIDDEN_BLOCK
    for t in range(steps + 2):
        if t < steps:
            part = slice(t * HIDDEN_BLOCK, (t + 1) * HIDDEN_BLOCK)
            pre[t % 2] = matmul(normed, w_up[:, part])
            dact[t % 2] = trans_right(grad, w_down[part, :])
        if 0 <= t - 1 < steps:
            part = slice((t - 1) * HIDDEN_BLOCK, t * HIDDEN_BLOCK)
            value, slope = gelu_parts(pre[(t - 1) % 2] + b_up[:, part])
            low = (dact[(t - 1) % 2] * slope).astype(BF)
            act[:, part] = value.astype(BF)
            gpre[:, part] = low
            db_up[:, part] = column_sum(low.astype(F32))
        if 0 <= t - 2 < steps:
            part = slice((t - 2) * HIDDEN_BLOCK, (t - 1) * HIDDEN_BLOCK)
            dw_down[part, :] = trans_left(act[:, part], grad).astype(BF)
            dw_up[:, part] = trans_left(normed, gpre[:, part]).astype(BF)
    grad_in = trans_right(gpre[...], w_up[...])
    dc0[...] = grad_in[:rows]
    dc1[...] = grad_in[rows:].astype(BF)
    out = matmul(act[...], w_down[...])
    out0[...] = out[:rows]
    out1[...] = out[rows:].astype(BF)


def feed(core, c0, c1, g0, g1, w_up, b_up, w_down):
    rows, width = c0.shape
    half = w_up.shape[1] // 2
    one, two = jax.ShapeDtypeStruct((rows, width), F32), jax.ShapeDtypeStruct((rows, width), BF)
    return call(
        feed_kernel,
        "feed",
        core,
        (c0, c1, g0, g1, w_up, b_up, w_down),
        [whole(rows, width)] * 4
        + [by_core((width, half), 1), by_core((1, half), 1), by_core((half, width), 0)],
        [
            jax.ShapeDtypeStruct((width, half), BF),
            jax.ShapeDtypeStruct((half, width), BF),
            jax.ShapeDtypeStruct((1, half), F32),
            one,
            two,
            one,
            two,
        ],
        [pltpu.VMEM((2, 2 * rows, HIDDEN_BLOCK), F32)] * 2 + [pltpu.VMEM((2 * rows, half), BF)] * 2,
        flops=2 * 6 * 2 * rows * width * half,
    )


def middle_back_kernel(core, h_ref, own, got, g_ref, gain, out, low, sums):
    normed, rscale = norm_forward(h_ref[...])
    grad_in = own[...] + got[...].astype(F32)
    upstream = g_ref[...].astype(F32)
    grad = upstream + norm_back(grad_in * gain[...], normed, rscale)
    out[...] = grad
    rounded = grad.astype(BF)
    low[...] = rounded
    sums[...] = jnp.concatenate(
        [
            column_sum(grad_in * normed),
            column_sum(grad_in),
            column_sum(rounded.astype(F32)),
            column_sum(upstream),
            jnp.zeros((4, sums.shape[1]), F32),
        ],
        axis=0,
    )


def middle_back(core, hidden1, own, got, grad, gain):
    rows, width = hidden1.shape
    return call(
        middle_back_kernel,
        "middle_back",
        core,
        (hidden1, own, got, grad, gain),
        [whole(rows, width)] * 4 + [whole(1, width)],
        [
            jax.ShapeDtypeStruct((rows, width), F32),
            jax.ShapeDtypeStruct((rows, width), BF),
            jax.ShapeDtypeStruct((8, width), F32),
        ],
    )


def mixed_back_kernel(core, g0, g1, mixed, w_out, grad_mixed, dw_out):
    grad = jnp.concatenate([g0[...], g1[...]], axis=0)
    grad_mixed[...] = trans_right(grad, w_out[...]).astype(BF)
    dw_out[...] = trans_left(mixed[...], grad).astype(BF)


def mixed_back(core, g0, g1, mixed, w_out):
    rows, width = g0.shape
    half = width // 2
    return call(
        mixed_back_kernel,
        "mixed_back",
        core,
        (g0, g1, mixed, w_out),
        [whole(rows, width)] * 2 + [whole(2 * rows, half), by_core((half, width), 0)],
        [jax.ShapeDtypeStruct((2 * rows, half), BF), jax.ShapeDtypeStruct((half, width), BF)],
        flops=2 * 2 * 2 * rows * width * half,
    )


def project_back_kernel(
    core, x0, x1, x2, x3, a0, a1, dq, dk, dv, wq, wk, wv, dwq, dwk, dwv, own, par, far, far_par, sums, qv_sums
):
    rows = x0.shape[0]
    near = 2 * rows
    a_near, a_far = a0[...], a1[...]
    dwq[...] = trans_left(a_near, dq[...]).astype(BF)
    dwk[...] = (trans_left(a_near, dk[:near]) + trans_left(a_far, dk[near:])).astype(BF)
    dwv[...] = (trans_left(a_near, dv[:near]) + trans_left(a_far, dv[near:])).astype(BF)
    chip = trans_right(dk[:near], wk[...]) + trans_right(dv[:near], wv[...]) + trans_right(dq[...], wq[...])
    away = trans_right(dk[near:], wk[...]) + trans_right(dv[near:], wv[...])
    own[...] = chip[:rows]
    par[...] = chip[rows:].astype(BF)
    far[...] = away[:rows]
    far_par[...] = away[rows:].astype(BF)
    gain = jnp.zeros((1, x0.shape[1]), F32)
    for x, terms in zip((x0, x1, x2, x3), (chip[:rows], chip[rows:], away[:rows], away[rows:])):
        normed, _ = norm_forward(x[...].astype(F32))
        gain = gain + column_sum(terms * normed)
    bias = column_sum(chip) + column_sum(away)
    sums[...] = jnp.concatenate([gain, bias, jnp.zeros((6, gain.shape[1]), F32)], axis=0)
    half = dq.shape[1]
    qv_sums[...] = jnp.concatenate(
        [
            column_sum(dq[...].astype(F32)),
            column_sum(dv[...].astype(F32)),
            jnp.zeros((6, half), F32),
        ],
        axis=0,
    )


def project_back(core, xs, attn_near, attn_far, dq, dk, dv, wq, wk, wv):
    rows, width = xs[0].shape
    half = width // 2
    weight = by_core((width, half), 1)
    grad = jax.ShapeDtypeStruct((width, half), BF)
    one, two = jax.ShapeDtypeStruct((rows, width), F32), jax.ShapeDtypeStruct((rows, width), BF)
    return call(
        project_back_kernel,
        "project_back",
        core,
        (*xs, attn_near, attn_far, dq, dk, dv, wq, wk, wv),
        [whole(rows, width)] * 4
        + [whole(2 * rows, width)] * 2
        + [whole(2 * rows, half), whole(4 * rows, half), whole(4 * rows, half)]
        + [weight] * 3,
        [grad] * 3
        + [one, two, one, two]
        + [jax.ShapeDtypeStruct((8, width), F32), jax.ShapeDtypeStruct((8, half), F32)],
        flops=2 * 10 * 2 * rows * width * half,
    )


def exchange(values, groups):
    return lax.all_to_all(values, BOTH, split_axis=0, concat_axis=0, axis_index_groups=groups)


def scatter_once(values, groups):
    rows, width = values.shape
    count = len(groups[0])
    got = exchange(values.reshape(count, rows // count, width), groups)
    return jnp.sum(got.astype(F32), axis=0).astype(BF)


def gather_once(piece, groups):
    few, width = piece.shape
    count = len(groups[0])
    got = exchange(jnp.broadcast_to(piece[None], (count, few, width)), groups)
    return got.reshape(count * few, width)


def per_device(
    tokens,
    lengths,
    ln1_gain,
    ln1_bias,
    w_query,
    b_query,
    w_key,
    w_value,
    b_value,
    w_out,
    b_out,
    ln2_gain,
    ln2_bias,
    w_up,
    b_up,
    w_down,
    b_down,
    cotangent,
):
    _, rows, width = tokens.shape
    hidden = w_up.shape[1]
    half = width // 2
    half_hidden = hidden // 2
    band = lax.axis_index("band")
    core = lax.rem(band, 2)
    is_first = core == 0
    core = core.reshape(1)
    flat = lambda values: values.reshape(1, -1)

    own = tokens.reshape(rows, width)
    grad_own = cotangent.reshape(rows, width)
    far = swap_z(own)
    par = swap_core(own)
    grad_par = swap_core(grad_own)
    far_par = swap_core(far)

    ends = jnp.cumsum(lengths[0])
    place = jnp.arange(rows, dtype=jnp.int32)
    slices = [band, band ^ 1, band ^ 2, band ^ 3]
    at_all = jnp.concatenate([s * rows + place for s in slices])
    seg_all = jnp.sum((at_all[:, None] >= ends[None, :]).astype(jnp.int32), axis=1)
    lanes = jnp.arange(SEGS, dtype=jnp.int32)
    count = lengths.shape[1]
    mask_q = (seg_all[None, : 2 * rows] == lanes[:, None]).astype(BF)
    mask_k = jnp.where(
        (seg_all[:, None] != lanes[None, :]) & (lanes[None, :] < count), -BARRED, 0.0
    ).astype(BF)

    params = (
        flat(ln1_gain),
        flat(ln1_bias),
        w_query,
        flat(b_query),
        w_key,
        w_value,
        flat(b_value),
    )
    attn_near, key_near, value_near, query = project(core, own, par, *params, True)
    attn_far, key_far, value_far = project(core, far, far_par, *params, False)
    mixed, lse = attend(core, query, key_near, key_far, value_near, value_far, mask_q, mask_k)
    mixed_other = swap_core(mixed[rows:])
    hidden1, mlp_own = middle(
        core, own, mixed[:rows], mixed_other, w_out, flat(b_out), flat(ln2_gain), flat(ln2_bias)
    )
    mlp_par = swap_core(mlp_own)
    dw_up, dw_down, db_up, out_own, out_par, dc_own, dc_par = feed(
        core, mlp_own, mlp_par, grad_own, grad_par, w_up, flat(b_up), w_down
    )
    dc_got = swap_core(dc_par)
    group_1 = jnp.concatenate([dw_up, dw_down[:width], dw_down[width:]], axis=1)
    part_1 = scatter_once(group_1, GROUPS_1)

    grad_hidden1, grad_attn, sums_2 = middle_back(
        core, hidden1, dc_own, dc_got, grad_own, flat(ln2_gain)
    )
    grad_attn_par = swap_core(grad_attn)
    grad_mixed, dw_out = mixed_back(core, grad_attn, grad_attn_par, mixed, w_out)
    dq, dk, dv = attend_back(
        core, query, key_near, key_far, value_near, value_far, mask_q, mask_k, mixed, grad_mixed, lse
    )
    dwq, dwk, dwv, t_own, t_par, t_far, t_far_par, sums_1, qv_sums = project_back(
        core, (own, par, far, far_par), attn_near, attn_far, dq, dk, dv, w_query, w_key, w_value
    )

    def widen(values):
        empty = jnp.zeros_like(values)
        return jnp.where(
            is_first,
            jnp.concatenate([values, empty], axis=1),
            jnp.concatenate([empty, values], axis=1),
        )

    vectors = jnp.concatenate(
        [sums_1[:2], widen(qv_sums[:2]), sums_2[:4], widen(db_up).reshape(4, width)], axis=0
    )
    group_2 = jnp.concatenate(
        [
            dwq,
            dwk,
            dwv,
            jnp.concatenate([dw_out[:, :half], dw_out[:, half:]], axis=0),
            vectors.T.astype(BF),
        ],
        axis=1,
    )
    piece_1 = scatter_once(part_1, GROUPS_2)
    piece_2 = scatter_once(group_2, GROUPS_ALL)
    total_2 = gather_once(piece_2, GROUPS_ALL)
    total_1 = gather_once(gather_once(piece_1, GROUPS_2), GROUPS_1)

    other_1 = swap_core(total_1)
    other_2 = swap_core(total_2)

    def joined(one, two, axis):
        one, two = one.astype(F32), two.astype(F32)
        first = jnp.where(is_first, one, two)
        second = jnp.where(is_first, two, one)
        return jnp.concatenate([first, second], axis=axis)

    def stacked(values):
        return jnp.concatenate([values[:, :width], values[:, width:]], axis=0)

    full_w_up = joined(total_1[:, :half_hidden], other_1[:, :half_hidden], 1)
    full_w_down = joined(stacked(total_1[:, half_hidden:]), stacked(other_1[:, half_hidden:]), 0)
    full_query, full_key, full_value = (
        joined(total_2[:, i * half : (i + 1) * half], other_2[:, i * half : (i + 1) * half], 1)
        for i in range(3)
    )

    def side_by_side(values):
        return jnp.concatenate([values[:half], values[half:]], axis=1)

    full_out = joined(
        side_by_side(total_2[:, 3 * half : 4 * half]),
        side_by_side(other_2[:, 3 * half : 4 * half]),
        0,
    )
    sides = (total_2[:, 4 * half :].astype(F32) + other_2[:, 4 * half :].astype(F32)).T
    full_b_up = sides[8:].reshape(hidden)

    got = swap_core(jnp.concatenate([t_par, t_far_par], axis=0)).astype(F32)
    far_terms = swap_z((t_far + got[rows:]).astype(BF)).astype(F32)
    normed1, rscale1 = norm_forward(own.astype(F32))
    grad_attn_in = t_own + got[:rows] + far_terms
    grad_tokens = grad_hidden1 + norm_back(grad_attn_in * ln1_gain, normed1, rscale1)
    layer_out = hidden1 + out_own + swap_core(out_par).astype(F32) + b_down
    return (
        layer_out.astype(BF)[None],
        grad_tokens[None],
        sides[0],
        sides[1],
        full_query,
        sides[2],
        full_key,
        full_value,
        sides[3],
        full_out,
        sides[6],
        sides[4],
        sides[5],
        full_w_up,
        full_b_up,
        full_w_down,
        sides[7],
    )


def solution(mesh):
    split = P("dp", "band", None)
    return jax.shard_map(
        per_device,
        mesh=mesh,
        in_specs=(split, P("dp", None)) + (P(),) * 15 + (split,),
        out_specs=(split, split) + (P(),) * 15,
        check_vma=False,
    )
```

```python
import functools

import jax
import jax.numpy as jnp
from jax import lax
from jax.experimental import pallas as pl
from jax.experimental.pallas import tpu as pltpu
from jax.sharding import PartitionSpec as P

HEADS = 12
HDIM = 64
PAIR = 2 * HDIM
SEGS = 128
BARRED = 2.0**100
BF = jnp.bfloat16
F32 = jnp.float32
BOTH = ("dp", "band")
CORE = [(0, 1), (1, 0), (2, 3), (3, 2)]
ZLO = [(0, 2), (1, 3), (2, 0), (3, 1)]
BIT_A = (0, 1, 1, 0)
BIT_B = (0, 0, 1, 1)
ONCE = pl.Buffered(1)
VMEM = {
    "near": 34,
    "far": 28,
    "attend_back": 56,
    "middle": 14,
    "feed": 32,
    "feed_weights": 30,
    "middle_back": 16,
    "project_back": 56,
    "finish_feed": 24,
    "finish_attend": 28,
    "finish_tokens": 16,
}


def place_of(device):
    dp, band = divmod(device, 4)
    x, rest = divmod(dp, 8)
    z_hi, y = divmod(rest, 4)
    z_lo, core = divmod(band, 2)
    return x, y, z_hi * 2 + z_lo, core


def cube_groups(first):
    groups = {}
    for device in range(128):
        x, y, z, core = place_of(device)
        fixed, moving = (BIT_B, BIT_A) if (core == 0) == first else (BIT_A, BIT_B)
        members = groups.setdefault((core, fixed[x], fixed[y], fixed[z]), [])
        members.append(((moving[x], moving[y], moving[z]), device))
    return [[device for _, device in sorted(members)] for members in groups.values()]


GROUPS_1 = cube_groups(True)
GROUPS_2 = cube_groups(False)


def matmul(left, right):
    return jnp.dot(left, right, preferred_element_type=F32)


def trans_left(left, right):
    return lax.dot_general(left, right, (((0,), (0,)), ((), ())), preferred_element_type=F32)


def trans_right(left, right):
    return lax.dot_general(left, right, (((1,), (1,)), ((), ())), preferred_element_type=F32)


def swap_core(values):
    return lax.ppermute(values, "band", CORE)


def swap_z(values):
    return lax.ppermute(values, "band", ZLO)


def norm_forward(values):
    centre = values - jnp.mean(values, axis=-1, keepdims=True)
    rscale = lax.rsqrt(jnp.mean(centre * centre, axis=-1, keepdims=True) + 1e-06)
    return centre * rscale, rscale


def norm_back(grad_norm, normed, rscale):
    first = jnp.mean(grad_norm, axis=-1, keepdims=True)
    second = jnp.mean(grad_norm * normed, axis=-1, keepdims=True)
    return rscale * (grad_norm - first - normed * second)


def column_sum(values):
    return jnp.sum(values, axis=0, keepdims=True)


def shape(dtype, *dims):
    return jax.ShapeDtypeStruct(dims, dtype)


def params(mebibytes):
    return pltpu.CompilerParams(vmem_limit_bytes=mebibytes * 2**20)


def whole(*dims):
    return pl.BlockSpec(dims, lambda i, core: (0,) * len(dims), pipeline_mode=ONCE)


def by_core(dims, axis):
    return pl.BlockSpec(
        dims,
        lambda i, core: tuple(core[0] if k == axis else 0 for k in range(len(dims))),
        pipeline_mode=ONCE,
    )


class Outgoing:
    def __init__(self, target, held, sem):
        self.target, self.held, self.sem, self.shape, self.copy = target, held, sem, held.shape, None

    def __setitem__(self, index, values):
        self.held[index] = values

    def __getitem__(self, index):
        return self.held[index]

    def send(self):
        self.copy = pltpu.make_async_copy(self.held, self.target, self.sem)
        self.copy.start()


def call(kernel, name, core, ins, in_specs, outs, vmem, scratch=(), flops=0, sent=(), pinned=()):
    first = len(ins)

    def body(core_ref, *refs):
        refs = list(refs)
        count = first + len(outs)
        held, sems = refs[count : count + len(sent)], refs[count + len(sent)] if sent else None
        own = refs[count + len(sent) + (1 if sent else 0) :]
        for k, i in enumerate(sent):
            refs[first + i] = Outgoing(refs[first + i], held[k], sems.at[k])
        kernel(core_ref, *refs[:count], *own)
        for i in sent:
            if refs[first + i].copy is None:
                refs[first + i].send()
        for i in sent:
            refs[first + i].copy.wait()

    holders = [pltpu.VMEM(outs[i].shape, outs[i].dtype) for i in sent]
    if sent:
        holders.append(pltpu.SemaphoreType.DMA((len(sent),)))
    traffic = sum(x.size * x.dtype.itemsize for x in list(ins) + list(outs))
    return pl.pallas_call(
        body,
        grid_spec=pltpu.PrefetchScalarGridSpec(
            num_scalar_prefetch=1,
            grid=(1,),
            in_specs=in_specs,
            out_specs=[
                pl.BlockSpec(memory_space=pltpu.HBM) if i in sent else whole(*x.shape)
                for i, x in enumerate(outs)
            ],
            scratch_shapes=holders + list(scratch),
        ),
        out_shape=[
            pltpu.HBM(x.shape, x.dtype) if i in sent or i in pinned else x for i, x in enumerate(outs)
        ],
        compiler_params=params(vmem),
        cost_estimate=pl.CostEstimate(flops=flops, bytes_accessed=traffic, transcendentals=0),
        name=name,
    )(core, *ins)


def in_hbm(values):
    return pltpu.with_memory_space_constraint(values, pltpu.HBM)


def core_half(core, vector):
    size = vector.shape[0] // 2
    values = vector[...]
    return jnp.where(core[0] == 0, values[:size], values[size:])[None, :]


def project_body(core, xs, weights, outs, with_query):
    gain, bias, wq, bq, wk, wv, bv = weights
    rows = xs[0].shape[0]
    for i, x in enumerate(xs):
        a_ref, k_ref, v_ref = outs[3 * i : 3 * i + 3]
        normed, _ = norm_forward(x[...].astype(F32))
        attn_in = (normed * gain[...][None, :] + bias[...][None, :]).astype(BF)
        a_ref[...] = attn_in
        k_ref[...] = matmul(attn_in, wk[...]).astype(BF)
        v_ref[...] = (matmul(attn_in, wv[...]) + core_half(core, bv)).astype(BF)
        if with_query:
            q_ref = outs[6 + i]
            q_ref[...] = (matmul(attn_in, wq[...]) + core_half(core, bq)).astype(BF) * 0.125


def head_rows(head, dims):
    return lax.broadcasted_iota(jnp.int32, dims, 0) // HDIM == head


def head_lanes(head, dims):
    return lax.broadcasted_iota(jnp.int32, dims, 1) // HDIM == head


KEY_BLOCK = 256
MAX_ROWS = 32


def attend_body(first, queries, keys, values, masks, before, outs, scratch):
    (q0, q1), (k0, k1), (v0, v1), (mq_ref, mk_ref) = queries, keys, values, masks
    s_buf, p_buf, rhs, vt, kx = scratch
    if first:
        o_ref, stat_ref = outs
    else:
        (o_ref, stat_ref), (mix0, mix1, lse_ref) = before, outs
    near, width = k0.shape
    rows_q = q0.shape[0]
    nq = 2 * rows_q
    nk = 2 * near
    heads = width // HDIM
    blocks = nk // KEY_BLOCK

    def prepare(head):
        pair = slice((head // 2) * PAIR, (head // 2 + 1) * PAIR)
        if head % 2 == 0:
            vt[(head // 2) % 2, :PAIR, :near] = v0[:, pair].T
            vt[(head // 2) % 2, :PAIR, near:] = v1[:, pair].T
            kx[(head // 2) % 2, :near, :PAIR] = k0[:, pair]
            kx[(head // 2) % 2, near:, :PAIR] = k1[:, pair]
        for at, ref in ((0, q0), (rows_q, q1)):
            turned = ref[:, pair].T
            rhs[head % 2, :PAIR, at : at + rows_q] = jnp.where(
                head_rows(head % 2, turned.shape), turned, jnp.zeros((), BF)
            )

    for i in range(2):
        vt[i, PAIR:] = jnp.ones((16, nk), BF)
        rhs[i, PAIR:] = mq_ref[...]
        kx[i, :, PAIR:] = mk_ref[...]
    peaks, outs, logs, norms = {}, [], [], []
    for t in range(heads + 2):
        if t < heads:
            prepare(t)
        peak, total = None, None
        for i in range(blocks):
            rows = slice(i * KEY_BLOCK, (i + 1) * KEY_BLOCK)
            if t < heads:
                scores = matmul(kx[(t // 2) % 2, rows, :], rhs[t % 2])
                s_buf[t % 2, rows, :] = scores
                for j in range(KEY_BLOCK // MAX_ROWS):
                    part = scores[j * MAX_ROWS : (j + 1) * MAX_ROWS]
                    peak = part if peak is None else jnp.maximum(peak, part)
            if 0 <= t - 1 < heads:
                p_buf[(t - 1) % 2, rows, :] = jnp.exp(
                    s_buf[(t - 1) % 2, rows, :] - peaks[t - 1]
                ).astype(BF)
            if 0 <= t - 2 < heads:
                part = matmul(vt[((t - 2) // 2) % 2, :, rows], p_buf[(t - 2) % 2, rows, :])
                total = part if total is None else total + part
        if t < heads:
            peaks[t] = jnp.max(peak, axis=0, keepdims=True)
            if not first:
                peaks[t] = jnp.maximum(peaks[t], stat_ref[t : t + 1, :])
        if 0 <= t - 2 < heads:
            head = t - 2
            side = head % 2
            own = slice(head * HDIM, (head + 1) * HDIM)
            norm = total[PAIR : PAIR + 1]
            mixed = total[side * HDIM : (side + 1) * HDIM]
            if first:
                o_ref[own, :] = mixed
                norms.append(norm)
                continue
            kept = jnp.exp(stat_ref[head : head + 1, :] - peaks[head])
            norm = norm + kept * stat_ref[8 + head : 9 + head, :]
            outs.append((mixed + kept * o_ref[own, :]) / norm)
            logs.append(peaks[head] + jnp.log(norm))
            if side == 1:
                pair = slice((head // 2) * PAIR, (head // 2 + 1) * PAIR)
                both = jnp.concatenate(outs[-2:], axis=0).T.astype(BF)
                mix0[:, pair] = both[:rows_q]
                mix1[:, pair] = both[rows_q:]
    spare = jnp.zeros((8 - heads, nq), F32)
    if first:
        stat_ref[...] = jnp.concatenate(
            [peaks[h] for h in range(heads)] + [spare] + norms + [spare], axis=0
        )
    else:
        for head in range(heads):
            lse_ref[head // 2, head % 2 : head % 2 + 1, :] = logs[head]


def near_kernel(core, *refs):
    xs, weights, masks = refs[:2], refs[2:9], refs[9:11]
    outs, tops, scratch = refs[11:19], refs[19:21], refs[21:]
    project_body(core, xs, weights, outs, True)
    for out in outs[:6]:
        out.send()
    a0, k0, v0, a1, k1, v1, q0, q1 = outs
    attend_body(True, (q0, q1), (k0, k1), (v0, v1), masks, None, tops, scratch)


def far_kernel(core, *refs):
    xs, weights, masks = refs[:2], refs[2:9], refs[9:11]
    queries, before, outs, tops, scratch = refs[11:13], refs[13:15], refs[15:21], refs[21:24], refs[24:]
    project_body(core, xs, weights, outs, False)
    for out in outs:
        out.send()
    a0, k0, v0, a1, k1, v1 = outs
    attend_body(False, queries, (k0, k1), (v0, v1), masks, before, tops, scratch)


def attend(core, xs, weights, masks, queries=(), before=()):
    rows, width = xs[0].shape
    half = width // 2
    heads = half // HDIM
    nq = nk = 2 * rows
    small = shape(BF, rows, half)
    outs = [shape(BF, rows, width), small, small] * 2
    if not before:
        outs += [small, small, shape(F32, half, nq), shape(F32, 16, nq)]
    else:
        outs += [small, small, shape(F32, heads // 2, 2, nq)]
    weight = by_core((width, half), 1)
    weights = [in_hbm(x) if x.ndim > 1 else x for x in weights]
    ins = (*xs, *weights, *masks, *queries, *before)
    return call(
        far_kernel if before else near_kernel,
        "attend",
        core,
        ins,
        [weight if x.shape == (width, width) else whole(*x.shape) for x in ins],
        outs,
        VMEM["far"] if before else VMEM["near"],
        [
            pltpu.VMEM((2, nk, nq), F32),
            pltpu.VMEM((2, nk, nq), BF),
            pltpu.VMEM((2, PAIR + SEGS, nq), BF),
            pltpu.VMEM((2, PAIR + 16, nk), BF),
            pltpu.VMEM((2, nk, PAIR + SEGS), BF),
        ],
        flops=2 * 2 * nq * nk * half * 4 + 2 * 2 * rows * width * half * 2,
        sent=tuple(range(6)) + ((8,) if before else ()),
    )


QUERY_BLOCK = 256


def attend_back_kernel(core, *refs):
    q0, q1, ks, vs = refs[0], refs[1], refs[2:6], refs[6:10]
    mq_ref, mk_ref, o0, o1, g0, g1, w_out, lse_ref, dq_ref, dk_ref, dv_ref, p_buf, ds_buf = refs[10:]
    nq = 2 * q0.shape[0]
    blocks = nq // QUERY_BLOCK
    nothing = jnp.zeros((), BF)
    upstream = jnp.concatenate([g0[...], g1[...]], axis=0)
    grad = trans_right(upstream, w_out[...]).astype(BF)
    query = jnp.concatenate([q0[...], q1[...]], axis=0)
    query_t, grad_t = query.T, grad.T
    key = jnp.concatenate([k[...] for k in ks], axis=0)
    value = jnp.concatenate([v[...] for v in vs], axis=0)
    key_t = key.T
    mixed = jnp.concatenate([o0[...], o1[...]], axis=0)
    product = grad_t.astype(F32) * mixed.T.astype(F32)
    key_masked = jnp.concatenate([key, mk_ref[...]], axis=1)
    mask_q = mq_ref[...]
    for b in range(blocks):
        cols = slice(b * QUERY_BLOCK, (b + 1) * QUERY_BLOCK)
        dqs = []
        for e in range(2):
            at = (e * blocks + b) * QUERY_BLOCK
            rows = head_rows(e, (PAIR, QUERY_BLOCK))
            query_e = jnp.where(rows, query_t[:, cols], nothing)
            grad_e = jnp.where(rows, grad_t[:, cols], nothing)
            scores = matmul(key_masked, jnp.concatenate([query_e, mask_q[:, cols]], axis=0))
            probs = jnp.exp(scores - lse_ref[0, e : e + 1, cols])
            p_buf[:, at : at + QUERY_BLOCK] = probs.astype(BF)
            grad_probs = matmul(value, grad_e)
            inner = jnp.sum(product[e * HDIM : (e + 1) * HDIM, cols], axis=0, keepdims=True)
            grad_scores = (probs * (grad_probs - inner)).astype(BF)
            ds_buf[:, at : at + QUERY_BLOCK] = grad_scores
            dqs.append(matmul(key_t, grad_scores)[e * HDIM : (e + 1) * HDIM])
        dq_ref[cols, :] = (jnp.concatenate(dqs, axis=0) * 0.125).T.astype(BF)

    def by_head(values):
        return jnp.concatenate(
            [jnp.where(head_lanes(e, values.shape), values, nothing) for e in range(2)], axis=0
        )

    dv_ref[...] = matmul(p_buf[...], by_head(grad)).astype(BF)
    dk_ref[...] = matmul(ds_buf[...], by_head(query)).astype(BF)


def attend_back(core, queries, keys, values, mask_q, mask_k, mixed, grads, w_out, lse):
    rows, width = queries[0].shape
    pairs = width // PAIR
    nq = 2 * rows
    nk = mask_k.shape[0]
    pair = lambda size: pl.BlockSpec((size, PAIR), lambda i, core: (0, i))
    outs = [shape(BF, size, width) for size in (nq, nk, nk)]
    ins = (*queries, *keys, *values, mask_q, mask_k, *mixed, *grads, w_out, lse)
    return pl.pallas_call(
        attend_back_kernel,
        grid_spec=pltpu.PrefetchScalarGridSpec(
            num_scalar_prefetch=1,
            grid=(pairs,),
            in_specs=[pair(rows)] * 10
            + [whole(SEGS, nq), whole(nk, SEGS)]
            + [pair(rows)] * 2
            + [whole(rows, 2 * width)] * 2
            + [pl.BlockSpec((PAIR, 2 * width), lambda i, core: (core[0] * pairs + i, 0))]
            + [pl.BlockSpec((1, 2, nq), lambda i, core: (i, 0, 0))],
            out_specs=[pair(nq), pair(nk), pair(nk)],
            scratch_shapes=[pltpu.VMEM((nk, 2 * nq), BF)] * 2,
        ),
        out_shape=outs,
        compiler_params=params(VMEM["attend_back"]),
        cost_estimate=pl.CostEstimate(
            flops=2 * 5 * nq * nk * width * 4,
            bytes_accessed=sum(x.size * x.dtype.itemsize for x in ins + tuple(outs)),
            transcendentals=0,
        ),
        name="attend_back",
    )(core, *ins)


def middle_kernel(core, x_ref, mine, other, w_out, b_out, gain, bias, h_ref, c_ref):
    half = mine.shape[1]
    at = pl.multiple_of(core[0] * half, 128)
    away = pl.multiple_of((1 - core[0]) * half, 128)
    hidden1 = x_ref[...].astype(F32) + (
        matmul(mine[...], w_out[pl.ds(at, half), :])
        + matmul(other[...], w_out[pl.ds(away, half), :])
        + b_out[...][None, :]
    )
    h_ref[...] = hidden1
    normed, _ = norm_forward(hidden1)
    c_ref[...] = (normed * gain[...][None, :] + bias[...][None, :]).astype(BF)


def middle(core, x, mine, other, w_out, b_out, gain, bias):
    rows, width = x.shape
    half = width // 2
    return call(
        middle_kernel,
        "middle",
        core,
        (x, mine, other, w_out, b_out, gain, bias),
        [whole(rows, width), whole(rows, half), whole(rows, half), whole(width, width)]
        + [whole(width)] * 3,
        [shape(F32, rows, width), shape(BF, rows, width)],
        VMEM["middle"],
        flops=2 * rows * width * width,
    )


HIDDEN_BLOCK = 512


def gelu_parts(values):
    bell = jnp.exp(values * values * -0.5)
    k = 1.0 / (1.0 + 0.23164188838 * jnp.abs(values))
    tail = 0.7107068705 + k * (-0.7265760135 + k * 0.5307027145)
    tail = k * (0.127414796 + k * (-0.142248368 + k * tail)) * bell
    below = jnp.where(values >= 0, 1.0 - tail, tail)
    return values * below, below + values * bell * 0.3989422804014327


def feed_kernel(core, c0, c1, g0, g1, w_up, b_up, w_down, act, gpre, db_up, dc0, dc1, pre, dact):
    rows = c0.shape[0]
    normed = jnp.concatenate([c0[...], c1[...]], axis=0)
    grad = jnp.concatenate([g0[...], g1[...]], axis=0)
    steps = w_up.shape[1] // HIDDEN_BLOCK
    bias = core_half(core, b_up)
    for t in range(steps + 1):
        if t < steps:
            part = slice(t * HIDDEN_BLOCK, (t + 1) * HIDDEN_BLOCK)
            pre[t % 2] = matmul(normed, w_up[:, part])
            dact[t % 2] = trans_right(grad, w_down[part, :])
        if t > 0:
            part = slice((t - 1) * HIDDEN_BLOCK, t * HIDDEN_BLOCK)
            value, slope = gelu_parts(pre[(t - 1) % 2] + bias[:, part])
            low = (dact[(t - 1) % 2] * slope).astype(BF)
            act[:, part] = value.astype(BF)
            gpre[:, part] = low
            db_up[:, part] = column_sum(low.astype(F32))
    grad_in = trans_right(gpre[...], w_up[...])
    dc0[...] = grad_in[:rows]
    dc1[...] = grad_in[rows:].astype(BF)


def feed(core, c0, c1, g0, g1, w_up, b_up, w_down):
    rows, width = c0.shape
    half = w_up.shape[1] // 2
    return call(
        feed_kernel,
        "feed",
        core,
        (c0, c1, g0, g1, w_up, b_up, w_down),
        [whole(rows, width)] * 4
        + [by_core((width, half), 1), whole(2 * half), by_core((half, width), 0)],
        [shape(BF, 2 * rows, half)] * 2
        + [shape(F32, 1, half), shape(F32, rows, width), shape(BF, rows, width)],
        VMEM["feed"],
        [pltpu.VMEM((2, 2 * rows, HIDDEN_BLOCK), F32)] * 2,
        pinned=(2,),
        flops=2 * 3 * 2 * rows * width * half,
    )


def feed_weights_kernel(core, c0, c1, g0, g1, act, gpre, w_down, dw, out0, out1):
    rows = c0.shape[0]
    normed = jnp.concatenate([c0[...], c1[...]], axis=0)
    grad = jnp.concatenate([g0[...], g1[...]], axis=0)
    hidden = act.shape[1]
    for t in range(hidden // HIDDEN_BLOCK):
        part = slice(t * HIDDEN_BLOCK, (t + 1) * HIDDEN_BLOCK)
        turned = slice(hidden + t * HIDDEN_BLOCK, hidden + (t + 1) * HIDDEN_BLOCK)
        dw[part, :] = trans_left(act[:, part], grad).astype(BF)
        dw[turned, :] = trans_left(gpre[:, part], normed).astype(BF)
    dw.send()
    out = matmul(act[...], w_down[...])
    out0[...] = out[:rows]
    out1[...] = out[rows:].astype(BF)


def feed_weights(core, c0, c1, g0, g1, act, gpre, w_down):
    rows, width = c0.shape
    half = act.shape[1]
    return call(
        feed_weights_kernel,
        "feed_weights",
        core,
        (c0, c1, g0, g1, act, gpre, w_down),
        [whole(rows, width)] * 4 + [whole(2 * rows, half)] * 2 + [by_core((half, width), 0)],
        [shape(BF, 2 * half, width), shape(F32, rows, width), shape(BF, rows, width)],
        VMEM["feed_weights"],
        sent=(0, 1, 2),
        flops=2 * 3 * 2 * rows * width * half,
    )


def middle_back_kernel(core, h_ref, own, got, g_ref, gain, out, low, sums):
    normed, rscale = norm_forward(h_ref[...])
    grad_in = own[...] + got[...].astype(F32)
    upstream = g_ref[...].astype(F32)
    grad = upstream + norm_back(grad_in * gain[...][None, :], normed, rscale)
    out[...] = grad
    rounded = grad.astype(BF)
    low[...] = rounded
    sums[...] = jnp.concatenate(
        [
            column_sum(grad_in * normed),
            column_sum(grad_in),
            column_sum(rounded.astype(F32)),
            column_sum(upstream),
            jnp.zeros((4, sums.shape[1]), F32),
        ],
        axis=0,
    )


def middle_back(core, hidden1, own, got, grad, gain):
    rows, width = hidden1.shape
    return call(
        middle_back_kernel,
        "middle_back",
        core,
        (hidden1, own, got, grad, gain),
        [whole(rows, width)] * 4 + [whole(width)],
        [shape(F32, rows, width), shape(BF, rows, width), shape(F32, 8, width)],
        VMEM["middle_back"],
        pinned=(0, 2),
    )


VECTORS = 16


def project_back_kernel(core, *refs):
    xs, attn, (dq, dk, dv, wq, wk, wv) = refs[:4], refs[4:8], refs[8:14]
    mix0, mix1, g0, g1, sums_2, db_up, grads, own, par, far, far_par = refs[14:]
    rows, width = xs[0].shape
    half = width // 2
    near = 2 * rows
    a_near = jnp.concatenate([attn[0][...], attn[1][...]], axis=0)
    a_all = jnp.concatenate([a_near, attn[2][...], attn[3][...]], axis=0)
    mixed = jnp.concatenate([mix0[...], mix1[...]], axis=0)
    upstream = jnp.concatenate([g0[...], g1[...]], axis=0)
    stacked = [
        trans_left(dq[...], a_near),
        trans_left(dk[...], a_all),
        trans_left(dv[...], a_all),
        trans_left(mixed, upstream),
    ]
    share = half // 2
    for i, block in enumerate(stacked):
        low = block.astype(BF)
        grads[2 * i, :share, :] = low[:share]
        grads[2 * i + 1, :share, :] = low[share:]
    chip = trans_right(dk[:near], wk[...]) + trans_right(dv[:near], wv[...]) + trans_right(dq[...], wq[...])
    away = trans_right(dk[near:], wk[...]) + trans_right(dv[near:], wv[...])
    parts = (chip[:rows], chip[rows:], away[:rows], away[rows:])
    own[...] = parts[0]
    par[...] = parts[1].astype(BF)
    far[...] = parts[2]
    far_par[...] = parts[3].astype(BF)
    gain = jnp.zeros((1, width), F32)
    for x, terms in zip(xs, parts):
        normed, _ = norm_forward(x[...].astype(F32))
        gain = gain + column_sum(terms * normed)
    bias = column_sum(chip) + column_sum(away)
    halves = jnp.concatenate(
        [column_sum(dq[...].astype(F32)), column_sum(dv[...].astype(F32))], axis=1
    )
    vectors = jnp.concatenate(
        [gain, bias, sums_2[0:4, :], db_up[:, :width], db_up[:, width:], halves]
        + [jnp.zeros((7, width), F32)],
        axis=0,
    ).astype(BF)
    for i in range(8):
        grads[i, share:, :] = vectors


def project_back(core, xs, attn, dq, dk, dv, wq, wk, wv, mixed, grads, sums_2, db_up):
    rows, width = xs[0].shape
    half = width // 2
    weight = by_core((width, half), 1)
    ins = (*xs, *attn, dq, dk, dv, wq, wk, wv, *mixed, *grads, sums_2, db_up)
    specs = [weight if x.shape == (width, width) else whole(*x.shape) for x in ins]
    return call(
        project_back_kernel,
        "project_back",
        core,
        ins,
        specs,
        [shape(BF, 8, width // 4 + VECTORS, width)]
        + [shape(F32, rows, width), shape(BF, rows, width)] * 2,
        VMEM["project_back"],
        flops=2 * 11 * 2 * rows * width * half,
    )


def finish_feed_kernel(core, mine_down, other_down, mine_up, other_up, w_down, w_up):
    ours = pl.program_id(0) == core[0]
    w_down[...] = jnp.where(ours, mine_down[0], other_down[0]).astype(F32)
    w_up[...] = jnp.where(ours, mine_up[0], other_up[0]).T.astype(F32)


def finish_feed(core, mine, other):
    _, block, width = mine.shape
    hidden = 8 * block

    def needed(half, first):
        def index(h, i, core):
            side = core[0] if half == 0 else 1 - core[0]
            at = jnp.where(h == side, i, jnp.where(h < side, 0, 3))
            return first + at, 0, 0

        return pl.BlockSpec((1, block, width), index)

    return pl.pallas_call(
        finish_feed_kernel,
        grid_spec=pltpu.PrefetchScalarGridSpec(
            num_scalar_prefetch=1,
            grid=(2, 4),
            in_specs=[needed(0, 0), needed(1, 0), needed(0, 4), needed(1, 4)],
            out_specs=[
                pl.BlockSpec((block, width), lambda h, i, core: (4 * h + i, 0)),
                pl.BlockSpec((width, block), lambda h, i, core: (0, 4 * h + i)),
            ],
        ),
        out_shape=[shape(F32, hidden, width), shape(F32, width, hidden)],
        compiler_params=params(VMEM["finish_feed"]),
        cost_estimate=pl.CostEstimate(flops=0, bytes_accessed=12 * hidden * width, transcendentals=0),
        name="finish_feed",
    )(core, mine, other, mine, other)


def finish_attend_kernel(core, mine, other, mine_vec, other_vec, wq, wk, wv, wo, *vecs):
    width = wq.shape[0]
    half = width // 2
    is_first = core[0] == 0
    for i, out in enumerate((wq, wk, wv, wo)):
        one, two = (
            jnp.concatenate([ref[2 * i], ref[2 * i + 1]], axis=0) for ref in (mine, other)
        )
        first = jnp.where(is_first, one, two)
        second = jnp.where(is_first, two, one)
        if i == 3:
            out[:half, :] = first.astype(F32)
            out[half:, :] = second.astype(F32)
        else:
            out[:, :half] = first.T.astype(F32)
            out[:, half:] = second.T.astype(F32)
    one, two = mine_vec[...].astype(F32), other_vec[...].astype(F32)
    both = one + two
    first = jnp.where(is_first, one, two)
    second = jnp.where(is_first, two, one)
    for k in range(6):
        vecs[k][...] = both[k]
    up, query_bias, value_bias = vecs[6:]
    up[...] = jnp.concatenate([first[6], first[7], second[6], second[7]], axis=0)
    query_bias[...] = jnp.concatenate([first[8, :half], second[8, :half]], axis=0)
    value_bias[...] = jnp.concatenate([first[8, half:], second[8, half:]], axis=0)


def finish_attend(core, mine, other, mine_vec, other_vec, width, hidden):
    outs = [shape(F32, width, width)] * 4 + [shape(F32, width)] * 6
    outs += [shape(F32, hidden), shape(F32, width), shape(F32, width)]
    ins = (mine, other, mine_vec, other_vec)
    return call(
        finish_attend_kernel,
        "finish_attend",
        core,
        ins,
        [whole(*x.shape) for x in ins],
        outs,
        VMEM["finish_attend"],
    )


def finish_tokens_kernel(core, x, own, got, far, hidden_grad, gain, out):
    normed, rscale = norm_forward(x[...].astype(F32))
    grad = own[...] + got[...].astype(F32) + far[...].astype(F32)
    out[...] = hidden_grad[...] + norm_back(grad * gain[...][None, :], normed, rscale)


def finish_tokens(core, x, own, got, far, hidden_grad, gain):
    rows, width = x.shape
    return call(
        finish_tokens_kernel,
        "finish_tokens",
        core,
        (x, own, got, far, hidden_grad, gain),
        [whole(rows, width)] * 5 + [whole(width)],
        [shape(F32, rows, width)],
        VMEM["finish_tokens"],
    )[0]


def exchange(values, groups):
    return lax.all_to_all(values, BOTH, split_axis=0, concat_axis=0, axis_index_groups=groups)


def add_up(got):
    return jnp.sum(got.astype(F32), axis=0).astype(BF)


def per_device(
    tokens,
    lengths,
    ln1_gain,
    ln1_bias,
    w_query,
    b_query,
    w_key,
    w_value,
    b_value,
    w_out,
    b_out,
    ln2_gain,
    ln2_bias,
    w_up,
    b_up,
    w_down,
    b_down,
    cotangent,
):
    _, rows, width = tokens.shape
    hidden = w_up.shape[1]
    band = lax.axis_index("band")
    core = lax.rem(band, 2).reshape(1)
    together = lax.optimization_barrier

    own = tokens.reshape(rows, width)
    grad_own = cotangent.reshape(rows, width)
    far = swap_z(own)
    par = swap_core(own)
    grad_par = swap_core(grad_own)

    ends = jnp.cumsum(lengths[0])
    place = jnp.arange(rows, dtype=jnp.int32)
    slices = [band, band ^ 1, band ^ 2, band ^ 3]
    at_all = jnp.concatenate([s * rows + place for s in slices])
    seg_all = jnp.sum((at_all[:, None] >= ends[None, :]).astype(jnp.int32), axis=1)
    lanes = jnp.arange(SEGS, dtype=jnp.int32)
    count = lengths.shape[1]
    mask_q = (seg_all[None, : 2 * rows] == lanes[:, None]).astype(BF)
    mask_k = jnp.where(
        (seg_all[:, None] != lanes[None, :]) & (lanes[None, :] < count), -BARRED, 0.0
    ).astype(BF)

    params = (ln1_gain, ln1_bias, w_query, b_query, w_key, w_value, b_value)
    *near, q0, q1, part, stats = attend(core, (own, par), params, (mask_q, mask_k[: 2 * rows]))
    queries, before = (q0, q1), (part, stats)
    far, before, grad_par = together((far, before, grad_par))
    far_par = swap_core(far)
    *away, mix_own, mix_par, lse = attend(
        core, (far, far_par), params, (mask_q, mask_k[2 * rows :]), queries, before
    )
    attn, keys, values = ((near[i], near[3 + i], away[i], away[3 + i]) for i in range(3))
    mix_other = swap_core(mix_par)
    hidden1, mlp_own = middle(core, own, mix_own, mix_other, w_out, b_out, ln2_gain, ln2_bias)
    mlp_par = swap_core(mlp_own)
    sides = (mlp_own, mlp_par, grad_own, grad_par)
    act, gpre, db_up, dc_own, dc_par = feed(core, *sides, w_up, b_up, w_down)
    dc_got = swap_core(dc_par)
    group_1, out_own, out_par = feed_weights(core, *sides, act, gpre, w_down)
    dc_got, group_1 = together((dc_got, group_1))
    dc_got = in_hbm(dc_got)
    grad_hidden1, grad_attn, sums_2 = middle_back(core, hidden1, dc_own, dc_got, grad_own, ln2_gain)
    grads = (grad_attn, swap_core(grad_attn))
    mixed = (mix_own, mix_par)
    got_1 = exchange(group_1.reshape(8, -1, width), GROUPS_1)
    dq, dk, dv = attend_back(
        core, queries, keys, values, mask_q, mask_k, mixed, grads, w_out, lse
    )
    group_2, t_own, t_par, t_far, t_far_par = project_back(
        core,
        (own, par, far, far_par),
        attn,
        dq,
        dk,
        dv,
        w_query,
        w_key,
        w_value,
        mixed,
        grads,
        sums_2,
        db_up,
    )
    got_1, group_2 = together((got_1, group_2))
    got_2 = exchange(group_2, GROUPS_1)
    part_1 = add_up(got_1)
    got_own, got_far = swap_core(t_par), swap_core(t_far_par)
    far_terms = swap_z((t_far + got_far.astype(F32)).astype(BF))
    layer_out = (hidden1 + out_own + swap_core(out_par).astype(F32) + b_down).astype(BF)
    got_2, part_1, layer_out = together((got_2, part_1, layer_out))
    part_2 = add_up(got_2)
    share = width // 4
    vectors = jnp.broadcast_to(part_2[None, share:], (8, VECTORS, width))
    both = [part_1.reshape(8, -1, width), part_2[:share].reshape(8, -1, width), vectors]
    piece = add_up(exchange(jnp.concatenate(both, axis=1), GROUPS_2))
    cut_1 = part_1.shape[0] // 8
    cut_2 = cut_1 + share // 8
    piece, far_terms = together((piece, far_terms))
    vectors = piece[cut_2:]
    got = exchange(jnp.broadcast_to(piece[None, :cut_2], (8, cut_2, width)), GROUPS_2)

    def spread(values):
        values = values.reshape(1, -1, width)
        return exchange(jnp.broadcast_to(values, (8,) + values.shape[1:]), GROUPS_1)

    grad_tokens = finish_tokens(core, own, t_own, got_own, far_terms, grad_hidden1, ln1_gain)
    total_1 = spread(got[:, :cut_1])
    got, total_1, grad_tokens = together((got, total_1, grad_tokens))
    total_2 = spread(got[:, cut_1:])
    other_1 = swap_core(total_1)
    other_vectors = swap_core(vectors)
    full_down, full_up = finish_feed(core, total_1, other_1)
    total_2, full_down, other_vectors = together((total_2, full_down, other_vectors))
    other_2 = swap_core(total_2)
    finished = finish_attend(core, total_2, other_2, vectors, other_vectors, width, hidden)
    full_query, full_key, full_value, full_out = finished[:4]
    d_gain1, d_bias1, d_gain2, d_bias2, d_b_out, d_b_down, d_b_up, d_b_query, d_b_value = finished[4:]
    return (
        layer_out[None],
        grad_tokens[None],
        d_gain1,
        d_bias1,
        full_query,
        d_b_query,
        full_key,
        full_value,
        d_b_value,
        full_out,
        d_b_out,
        d_gain2,
        d_bias2,
        full_up,
        d_b_up,
        full_down,
        d_b_down,
    )


def solution(mesh):
    split = P("dp", "band", None)
    return jax.shard_map(
        per_device,
        mesh=mesh,
        in_specs=(split, P("dp", None)) + (P(),) * 15 + (split,),
        out_specs=(split, split) + (P(),) * 15,
        check_vma=False,
    )
```

```python
import functools

import jax
import jax.numpy as jnp
from jax import lax
from jax.experimental import pallas as pl
from jax.experimental.pallas import tpu as pltpu
from jax.sharding import PartitionSpec as P

HEADS = 12
HDIM = 64
PAIR = 2 * HDIM
SEGS = 128
BARRED = 2.0**100
BF = jnp.bfloat16
F32 = jnp.float32
BOTH = ("dp", "band")
CORE = [(0, 1), (1, 0), (2, 3), (3, 2)]
ZLO = [(0, 2), (1, 3), (2, 0), (3, 1)]
BIT_A = (0, 1, 1, 0)
BIT_B = (0, 0, 1, 1)
ONCE = pl.Buffered(1)
VMEM = {
    "near": 34,
    "far": 28,
    "attend_back": 56,
    "middle": 14,
    "feed": 32,
    "feed_weights": 30,
    "feed_out": 30,
    "add_up": 24,
    "middle_back": 16,
    "weights_back": 56,
    "terms_back": 56,
    "finish_feed": 24,
    "finish_attend": 28,
    "finish_tokens": 16,
}


def place_of(device):
    dp, band = divmod(device, 4)
    x, rest = divmod(dp, 8)
    z_hi, y = divmod(rest, 4)
    z_lo, core = divmod(band, 2)
    return x, y, z_hi * 2 + z_lo, core


def cube_groups(first):
    groups = {}
    for device in range(128):
        x, y, z, core = place_of(device)
        fixed, moving = (BIT_B, BIT_A) if (core == 0) == first else (BIT_A, BIT_B)
        members = groups.setdefault((core, fixed[x], fixed[y], fixed[z]), [])
        members.append(((moving[x], moving[y], moving[z]), device))
    return [[device for _, device in sorted(members)] for members in groups.values()]


GROUPS_1 = cube_groups(True)


def matmul(left, right):
    return jnp.dot(left, right, preferred_element_type=F32)


def trans_left(left, right):
    return lax.dot_general(left, right, (((0,), (0,)), ((), ())), preferred_element_type=F32)


def trans_right(left, right):
    return lax.dot_general(left, right, (((1,), (1,)), ((), ())), preferred_element_type=F32)


def swap_core(values):
    return lax.ppermute(values, "band", CORE)


def swap_z(values):
    return lax.ppermute(values, "band", ZLO)


def norm_forward(values):
    centre = values - jnp.mean(values, axis=-1, keepdims=True)
    rscale = lax.rsqrt(jnp.mean(centre * centre, axis=-1, keepdims=True) + 1e-06)
    return centre * rscale, rscale


def norm_back(grad_norm, normed, rscale):
    first = jnp.mean(grad_norm, axis=-1, keepdims=True)
    second = jnp.mean(grad_norm * normed, axis=-1, keepdims=True)
    return rscale * (grad_norm - first - normed * second)


def column_sum(values):
    return jnp.sum(values, axis=0, keepdims=True)


def shape(dtype, *dims):
    return jax.ShapeDtypeStruct(dims, dtype)


def params(mebibytes):
    return pltpu.CompilerParams(vmem_limit_bytes=mebibytes * 2**20)


def whole(*dims):
    return pl.BlockSpec(dims, lambda i, core: (0,) * len(dims), pipeline_mode=ONCE)


def by_core(dims, axis):
    return pl.BlockSpec(
        dims,
        lambda i, core: tuple(core[0] if k == axis else 0 for k in range(len(dims))),
        pipeline_mode=ONCE,
    )


class Outgoing:
    def __init__(self, target, held, sem):
        self.target, self.held, self.sem, self.shape, self.copy = target, held, sem, held.shape, None

    def __setitem__(self, index, values):
        self.held[index] = values

    def __getitem__(self, index):
        return self.held[index]

    def send(self):
        self.copy = pltpu.make_async_copy(self.held, self.target, self.sem)
        self.copy.start()


def call(kernel, name, core, ins, in_specs, outs, vmem, scratch=(), flops=0, sent=(), pinned=()):
    first = len(ins)

    def body(core_ref, *refs):
        refs = list(refs)
        count = first + len(outs)
        held, sems = refs[count : count + len(sent)], refs[count + len(sent)] if sent else None
        own = refs[count + len(sent) + (1 if sent else 0) :]
        for k, i in enumerate(sent):
            refs[first + i] = Outgoing(refs[first + i], held[k], sems.at[k])
        kernel(core_ref, *refs[:count], *own)
        for i in sent:
            if refs[first + i].copy is None:
                refs[first + i].send()
        for i in sent:
            refs[first + i].copy.wait()

    holders = [pltpu.VMEM(outs[i].shape, outs[i].dtype) for i in sent]
    if sent:
        holders.append(pltpu.SemaphoreType.DMA((len(sent),)))
    traffic = sum(x.size * x.dtype.itemsize for x in list(ins) + list(outs))
    return pl.pallas_call(
        body,
        grid_spec=pltpu.PrefetchScalarGridSpec(
            num_scalar_prefetch=1,
            grid=(1,),
            in_specs=in_specs,
            out_specs=[
                pl.BlockSpec(memory_space=pltpu.HBM) if i in sent else whole(*x.shape)
                for i, x in enumerate(outs)
            ],
            scratch_shapes=holders + list(scratch),
        ),
        out_shape=[
            pltpu.HBM(x.shape, x.dtype) if i in sent or i in pinned else x for i, x in enumerate(outs)
        ],
        compiler_params=params(vmem),
        cost_estimate=pl.CostEstimate(flops=flops, bytes_accessed=traffic, transcendentals=0),
        name=name,
    )(core, *ins)


def in_hbm(values):
    return pltpu.with_memory_space_constraint(values, pltpu.HBM)


def core_half(core, vector):
    size = vector.shape[0] // 2
    values = vector[...]
    return jnp.where(core[0] == 0, values[:size], values[size:])[None, :]


def project_body(core, xs, weights, outs, with_query):
    gain, bias, wq, bq, wk, wv, bv = weights
    rows = xs[0].shape[0]
    for i, x in enumerate(xs):
        a_ref, k_ref, v_ref = outs[3 * i : 3 * i + 3]
        normed, _ = norm_forward(x[...].astype(F32))
        attn_in = (normed * gain[...][None, :] + bias[...][None, :]).astype(BF)
        a_ref[...] = attn_in
        k_ref[...] = matmul(attn_in, wk[...]).astype(BF)
        v_ref[...] = (matmul(attn_in, wv[...]) + core_half(core, bv)).astype(BF)
        if with_query:
            q_ref = outs[6 + i]
            q_ref[...] = (matmul(attn_in, wq[...]) + core_half(core, bq)).astype(BF) * 0.125


def head_rows(head, dims):
    return lax.broadcasted_iota(jnp.int32, dims, 0) // HDIM == head


def head_lanes(head, dims):
    return lax.broadcasted_iota(jnp.int32, dims, 1) // HDIM == head


KEY_BLOCK = 256
MAX_ROWS = 32


def attend_body(first, queries, keys, values, masks, before, outs, scratch):
    (q0, q1), (k0, k1), (v0, v1), (mq_ref, mk_ref) = queries, keys, values, masks
    s_buf, p_buf, rhs, vt, kx = scratch
    if first:
        o_ref, stat_ref = outs
    else:
        (o_ref, stat_ref), (mix0, mix1, lse_ref) = before, outs
    near, width = k0.shape
    rows_q = q0.shape[0]
    nq = 2 * rows_q
    nk = 2 * near
    heads = width // HDIM
    blocks = nk // KEY_BLOCK

    def prepare(head):
        pair = slice((head // 2) * PAIR, (head // 2 + 1) * PAIR)
        if head % 2 == 0:
            vt[(head // 2) % 2, :PAIR, :near] = v0[:, pair].T
            vt[(head // 2) % 2, :PAIR, near:] = v1[:, pair].T
            kx[(head // 2) % 2, :near, :PAIR] = k0[:, pair]
            kx[(head // 2) % 2, near:, :PAIR] = k1[:, pair]
        for at, ref in ((0, q0), (rows_q, q1)):
            turned = ref[:, pair].T
            rhs[head % 2, :PAIR, at : at + rows_q] = jnp.where(
                head_rows(head % 2, turned.shape), turned, jnp.zeros((), BF)
            )

    for i in range(2):
        vt[i, PAIR:] = jnp.ones((16, nk), BF)
        rhs[i, PAIR:] = mq_ref[...]
        kx[i, :, PAIR:] = mk_ref[...]
    peaks, outs, logs, norms = {}, [], [], []
    for t in range(heads + 2):
        if t < heads:
            prepare(t)
        peak, total = None, None
        for i in range(blocks):
            rows = slice(i * KEY_BLOCK, (i + 1) * KEY_BLOCK)
            if t < heads:
                scores = matmul(kx[(t // 2) % 2, rows, :], rhs[t % 2])
                s_buf[t % 2, rows, :] = scores
                for j in range(KEY_BLOCK // MAX_ROWS):
                    part = scores[j * MAX_ROWS : (j + 1) * MAX_ROWS]
                    peak = part if peak is None else jnp.maximum(peak, part)
            if 0 <= t - 1 < heads:
                p_buf[(t - 1) % 2, rows, :] = jnp.exp(
                    s_buf[(t - 1) % 2, rows, :] - peaks[t - 1]
                ).astype(BF)
            if 0 <= t - 2 < heads:
                part = matmul(vt[((t - 2) // 2) % 2, :, rows], p_buf[(t - 2) % 2, rows, :])
                total = part if total is None else total + part
        if t < heads:
            peaks[t] = jnp.max(peak, axis=0, keepdims=True)
            if not first:
                peaks[t] = jnp.maximum(peaks[t], stat_ref[t : t + 1, :])
        if 0 <= t - 2 < heads:
            head = t - 2
            side = head % 2
            own = slice(head * HDIM, (head + 1) * HDIM)
            norm = total[PAIR : PAIR + 1]
            mixed = total[side * HDIM : (side + 1) * HDIM]
            if first:
                o_ref[own, :] = mixed
                norms.append(norm)
                continue
            kept = jnp.exp(stat_ref[head : head + 1, :] - peaks[head])
            norm = norm + kept * stat_ref[8 + head : 9 + head, :]
            outs.append((mixed + kept * o_ref[own, :]) / norm)
            logs.append(peaks[head] + jnp.log(norm))
            if side == 1:
                pair = slice((head // 2) * PAIR, (head // 2 + 1) * PAIR)
                both = jnp.concatenate(outs[-2:], axis=0).T.astype(BF)
                mix0[:, pair] = both[:rows_q]
                mix1[:, pair] = both[rows_q:]
    spare = jnp.zeros((8 - heads, nq), F32)
    if first:
        stat_ref[...] = jnp.concatenate(
            [peaks[h] for h in range(heads)] + [spare] + norms + [spare], axis=0
        )
    else:
        for head in range(heads):
            lse_ref[head // 2, head % 2 : head % 2 + 1, :] = logs[head]


def near_kernel(core, *refs):
    xs, weights, masks = refs[:2], refs[2:9], refs[9:11]
    outs, tops, scratch = refs[11:19], refs[19:21], refs[21:]
    project_body(core, xs, weights, outs, True)
    for out in outs[:6]:
        out.send()
    a0, k0, v0, a1, k1, v1, q0, q1 = outs
    attend_body(True, (q0, q1), (k0, k1), (v0, v1), masks, None, tops, scratch)


def far_kernel(core, *refs):
    xs, weights, masks = refs[:2], refs[2:9], refs[9:11]
    queries, before, outs, tops, scratch = refs[11:13], refs[13:15], refs[15:21], refs[21:24], refs[24:]
    project_body(core, xs, weights, outs, False)
    for out in outs:
        out.send()
    a0, k0, v0, a1, k1, v1 = outs
    attend_body(False, queries, (k0, k1), (v0, v1), masks, before, tops, scratch)


def attend(core, xs, weights, masks, queries=(), before=()):
    rows, width = xs[0].shape
    half = width // 2
    heads = half // HDIM
    nq = nk = 2 * rows
    small = shape(BF, rows, half)
    outs = [shape(BF, rows, width), small, small] * 2
    if not before:
        outs += [small, small, shape(F32, half, nq), shape(F32, 16, nq)]
    else:
        outs += [small, small, shape(F32, heads // 2, 2, nq)]
    weight = by_core((width, half), 1)
    weights = [in_hbm(x) if x.ndim > 1 else x for x in weights]
    ins = (*xs, *weights, *masks, *queries, *before)
    return call(
        far_kernel if before else near_kernel,
        "attend",
        core,
        ins,
        [weight if x.shape == (width, width) else whole(*x.shape) for x in ins],
        outs,
        VMEM["far"] if before else VMEM["near"],
        [
            pltpu.VMEM((2, nk, nq), F32),
            pltpu.VMEM((2, nk, nq), BF),
            pltpu.VMEM((2, PAIR + SEGS, nq), BF),
            pltpu.VMEM((2, PAIR + 16, nk), BF),
            pltpu.VMEM((2, nk, PAIR + SEGS), BF),
        ],
        flops=2 * 2 * nq * nk * half * 4 + 2 * 2 * rows * width * half * 2,
        sent=tuple(range(6)) + ((8,) if before else ()),
    )


QUERY_BLOCK = 256


def attend_back_kernel(core, *refs):
    q0, q1, ks, vs = refs[0], refs[1], refs[2:6], refs[6:10]
    mq_ref, mk_ref, o0, o1, g0, g1, w_out, lse_ref, dq_ref, dk_ref, dv_ref, p_buf, ds_buf = refs[10:]
    nq = 2 * q0.shape[0]
    blocks = nq // QUERY_BLOCK
    nothing = jnp.zeros((), BF)
    upstream = jnp.concatenate([g0[...], g1[...]], axis=0)
    grad = trans_right(upstream, w_out[...]).astype(BF)
    query = jnp.concatenate([q0[...], q1[...]], axis=0)
    query_t, grad_t = query.T, grad.T
    key = jnp.concatenate([k[...] for k in ks], axis=0)
    value = jnp.concatenate([v[...] for v in vs], axis=0)
    key_t = key.T
    mixed = jnp.concatenate([o0[...], o1[...]], axis=0)
    product = grad_t.astype(F32) * mixed.T.astype(F32)
    key_masked = jnp.concatenate([key, mk_ref[...]], axis=1)
    mask_q = mq_ref[...]
    for b in range(blocks):
        cols = slice(b * QUERY_BLOCK, (b + 1) * QUERY_BLOCK)
        dqs = []
        for e in range(2):
            at = (e * blocks + b) * QUERY_BLOCK
            rows = head_rows(e, (PAIR, QUERY_BLOCK))
            query_e = jnp.where(rows, query_t[:, cols], nothing)
            grad_e = jnp.where(rows, grad_t[:, cols], nothing)
            scores = matmul(key_masked, jnp.concatenate([query_e, mask_q[:, cols]], axis=0))
            probs = jnp.exp(scores - lse_ref[0, e : e + 1, cols])
            p_buf[:, at : at + QUERY_BLOCK] = probs.astype(BF)
            grad_probs = matmul(value, grad_e)
            inner = jnp.sum(product[e * HDIM : (e + 1) * HDIM, cols], axis=0, keepdims=True)
            grad_scores = (probs * (grad_probs - inner)).astype(BF)
            ds_buf[:, at : at + QUERY_BLOCK] = grad_scores
            dqs.append(matmul(key_t, grad_scores)[e * HDIM : (e + 1) * HDIM])
        dq_ref[cols, :] = (jnp.concatenate(dqs, axis=0) * 0.125).T.astype(BF)

    def by_head(values):
        return jnp.concatenate(
            [jnp.where(head_lanes(e, values.shape), values, nothing) for e in range(2)], axis=0
        )

    dv_ref[...] = matmul(p_buf[...], by_head(grad)).astype(BF)
    dk_ref[...] = matmul(ds_buf[...], by_head(query)).astype(BF)


def attend_back(core, queries, keys, values, mask_q, mask_k, mixed, grads, w_out, lse):
    rows, width = queries[0].shape
    pairs = width // PAIR
    nq = 2 * rows
    nk = mask_k.shape[0]
    pair = lambda size: pl.BlockSpec((size, PAIR), lambda i, core: (0, i))
    outs = [shape(BF, size, width) for size in (nq, nk, nk)]
    ins = (*queries, *keys, *values, mask_q, mask_k, *mixed, *grads, w_out, lse)
    return pl.pallas_call(
        attend_back_kernel,
        grid_spec=pltpu.PrefetchScalarGridSpec(
            num_scalar_prefetch=1,
            grid=(pairs,),
            in_specs=[pair(rows)] * 10
            + [whole(SEGS, nq), whole(nk, SEGS)]
            + [pair(rows)] * 2
            + [whole(rows, 2 * width)] * 2
            + [pl.BlockSpec((PAIR, 2 * width), lambda i, core: (core[0] * pairs + i, 0))]
            + [pl.BlockSpec((1, 2, nq), lambda i, core: (i, 0, 0))],
            out_specs=[pair(nq), pair(nk), pair(nk)],
            scratch_shapes=[pltpu.VMEM((nk, 2 * nq), BF)] * 2,
        ),
        out_shape=outs,
        compiler_params=params(VMEM["attend_back"]),
        cost_estimate=pl.CostEstimate(
            flops=2 * 5 * nq * nk * width * 4,
            bytes_accessed=sum(x.size * x.dtype.itemsize for x in ins + tuple(outs)),
            transcendentals=0,
        ),
        name="attend_back",
    )(core, *ins)


def middle_kernel(core, x_ref, mine, other, w_out, b_out, gain, bias, h_ref, c_ref):
    half = mine.shape[1]
    at = pl.multiple_of(core[0] * half, 128)
    away = pl.multiple_of((1 - core[0]) * half, 128)
    hidden1 = x_ref[...].astype(F32) + (
        matmul(mine[...], w_out[pl.ds(at, half), :])
        + matmul(other[...], w_out[pl.ds(away, half), :])
        + b_out[...][None, :]
    )
    h_ref[...] = hidden1
    normed, _ = norm_forward(hidden1)
    c_ref[...] = (normed * gain[...][None, :] + bias[...][None, :]).astype(BF)


def middle(core, x, mine, other, w_out, b_out, gain, bias):
    rows, width = x.shape
    half = width // 2
    return call(
        middle_kernel,
        "middle",
        core,
        (x, mine, other, w_out, b_out, gain, bias),
        [whole(rows, width), whole(rows, half), whole(rows, half), whole(width, width)]
        + [whole(width)] * 3,
        [shape(F32, rows, width), shape(BF, rows, width)],
        VMEM["middle"],
        flops=2 * rows * width * width,
    )


HIDDEN_BLOCK = 512


def gelu_parts(values):
    bell = jnp.exp(values * values * -0.5)
    k = 1.0 / (1.0 + 0.23164188838 * jnp.abs(values))
    tail = 0.7107068705 + k * (-0.7265760135 + k * 0.5307027145)
    tail = k * (0.127414796 + k * (-0.142248368 + k * tail)) * bell
    below = jnp.where(values >= 0, 1.0 - tail, tail)
    return values * below, below + values * bell * 0.3989422804014327


def feed_kernel(core, c0, c1, g0, g1, w_up, b_up, w_down, act, gpre, db_up, dc0, dc1, pre, dact):
    rows = c0.shape[0]
    normed = jnp.concatenate([c0[...], c1[...]], axis=0)
    grad = jnp.concatenate([g0[...], g1[...]], axis=0)
    steps = w_up.shape[1] // HIDDEN_BLOCK
    bias = core_half(core, b_up)
    for t in range(steps + 1):
        if t < steps:
            part = slice(t * HIDDEN_BLOCK, (t + 1) * HIDDEN_BLOCK)
            pre[t % 2] = matmul(normed, w_up[:, part])
            dact[t % 2] = trans_right(grad, w_down[part, :])
        if t > 0:
            part = slice((t - 1) * HIDDEN_BLOCK, t * HIDDEN_BLOCK)
            value, slope = gelu_parts(pre[(t - 1) % 2] + bias[:, part])
            low = (dact[(t - 1) % 2] * slope).astype(BF)
            act[:, part] = value.astype(BF)
            gpre[:, part] = low
            db_up[:, part] = column_sum(low.astype(F32))
    grad_in = trans_right(gpre[...], w_up[...])
    dc0[...] = grad_in[:rows]
    dc1[...] = grad_in[rows:].astype(BF)


def feed(core, c0, c1, g0, g1, w_up, b_up, w_down):
    rows, width = c0.shape
    half = w_up.shape[1] // 2
    return call(
        feed_kernel,
        "feed",
        core,
        (c0, c1, g0, g1, w_up, b_up, w_down),
        [whole(rows, width)] * 4
        + [by_core((width, half), 1), whole(2 * half), by_core((half, width), 0)],
        [shape(BF, 2 * rows, half)] * 2
        + [shape(F32, 1, half), shape(F32, rows, width), shape(BF, rows, width)],
        VMEM["feed"],
        [pltpu.VMEM((2, 2 * rows, HIDDEN_BLOCK), F32)] * 2,
        pinned=(2,),
        flops=2 * 3 * 2 * rows * width * half,
    )


def feed_weights_kernel(core, c0, c1, g0, g1, act, gpre, dw_out, dw, sems):
    normed = jnp.concatenate([c0[...], c1[...]], axis=0)
    grad = jnp.concatenate([g0[...], g1[...]], axis=0)
    hidden = act.shape[1]
    copies = []
    for t in range(hidden // HIDDEN_BLOCK):
        part = slice(t * HIDDEN_BLOCK, (t + 1) * HIDDEN_BLOCK)
        turned = slice(hidden + t * HIDDEN_BLOCK, hidden + (t + 1) * HIDDEN_BLOCK)
        dw[part, :] = trans_left(act[:, part], grad).astype(BF)
        dw[turned, :] = trans_left(gpre[:, part], normed).astype(BF)
        for k, span in enumerate((part, turned)):
            copies.append(
                pltpu.make_async_copy(dw.at[span, :], dw_out.at[span, :], sems.at[2 * t + k])
            )
            copies[-1].start()
    for copy in copies:
        copy.wait()


def feed_weights(core, c0, c1, g0, g1, act, gpre):
    rows, width = c0.shape
    half = act.shape[1]
    ins = (c0, c1, g0, g1, act, gpre)
    return pl.pallas_call(
        feed_weights_kernel,
        grid_spec=pltpu.PrefetchScalarGridSpec(
            num_scalar_prefetch=1,
            grid=(1,),
            in_specs=[whole(*x.shape) for x in ins],
            out_specs=pl.BlockSpec(memory_space=pltpu.HBM),
            scratch_shapes=[
                pltpu.VMEM((2 * half, width), BF),
                pltpu.SemaphoreType.DMA((2 * half // HIDDEN_BLOCK,)),
            ],
        ),
        out_shape=pltpu.HBM((2 * half, width), BF),
        compiler_params=params(VMEM["feed_weights"]),
        cost_estimate=pl.CostEstimate(
            flops=2 * 2 * 2 * rows * width * half,
            bytes_accessed=2 * (4 * rows * width + 4 * rows * half + 2 * half * width),
            transcendentals=0,
        ),
        name="feed_weights",
    )(core, *ins)


def feed_out_kernel(core, act, w_down, out0, out1):
    rows = out0.shape[0]
    out = matmul(act[...], w_down[...])
    out0[...] = out[:rows]
    out1[...] = out[rows:].astype(BF)


def feed_out(core, act, w_down):
    rows, half = act.shape[0] // 2, act.shape[1]
    width = w_down.shape[1]
    return call(
        feed_out_kernel,
        "feed_out",
        core,
        (act, w_down),
        [whole(2 * rows, half), by_core((half, width), 0)],
        [shape(F32, rows, width), shape(BF, rows, width)],
        VMEM["feed_out"],
        flops=2 * 2 * rows * width * half,
    )


def middle_back_kernel(core, h_ref, own, got, g_ref, gain, out, low, sums):
    normed, rscale = norm_forward(h_ref[...])
    grad_in = own[...] + got[...].astype(F32)
    upstream = g_ref[...].astype(F32)
    grad = upstream + norm_back(grad_in * gain[...][None, :], normed, rscale)
    out[...] = grad
    rounded = grad.astype(BF)
    low[...] = rounded
    sums[...] = jnp.concatenate(
        [
            column_sum(grad_in * normed),
            column_sum(grad_in),
            column_sum(rounded.astype(F32)),
            column_sum(upstream),
            jnp.zeros((4, sums.shape[1]), F32),
        ],
        axis=0,
    )


def middle_back(core, hidden1, own, got, grad, gain):
    rows, width = hidden1.shape
    return call(
        middle_back_kernel,
        "middle_back",
        core,
        (hidden1, own, got, grad, gain),
        [whole(rows, width)] * 4 + [whole(width)],
        [shape(F32, rows, width), shape(BF, rows, width), shape(F32, 8, width)],
        VMEM["middle_back"],
        pinned=(0, 2),
    )


VECTORS = 16


def weights_back_kernel(core, *refs):
    attn, (dq, dk, dv, mix0, mix1, g0, g1, sums_2, db_up, grads) = refs[:4], refs[4:]
    rows, width = attn[0].shape
    half = width // 2
    a_near = jnp.concatenate([attn[0][...], attn[1][...]], axis=0)
    a_all = jnp.concatenate([a_near, attn[2][...], attn[3][...]], axis=0)
    mixed = jnp.concatenate([mix0[...], mix1[...]], axis=0)
    upstream = jnp.concatenate([g0[...], g1[...]], axis=0)
    stacked = [
        trans_left(dq[...], a_near),
        trans_left(dk[...], a_all),
        trans_left(dv[...], a_all),
        trans_left(mixed, upstream),
    ]
    share = half // 2
    for i, block in enumerate(stacked):
        low = block.astype(BF)
        grads[2 * i, :share, :] = low[:share]
        grads[2 * i + 1, :share, :] = low[share:]
    halves = jnp.concatenate(
        [column_sum(dq[...].astype(F32)), column_sum(dv[...].astype(F32))], axis=1
    )
    vectors = jnp.concatenate(
        [sums_2[0:4, :], db_up[:, :width], db_up[:, width:], halves]
        + [jnp.zeros((VECTORS - 7, width), F32)],
        axis=0,
    ).astype(BF)
    for i in range(8):
        grads[i, share:, :] = vectors


def weights_back(core, attn, dq, dk, dv, mixed, grads, sums_2, db_up):
    rows, width = attn[0].shape
    half = width // 2
    ins = (*attn, dq, dk, dv, *mixed, *grads, sums_2, db_up)
    return call(
        weights_back_kernel,
        "weights_back",
        core,
        ins,
        [whole(*x.shape) for x in ins],
        [shape(BF, 8, width // 4 + VECTORS, width)],
        VMEM["weights_back"],
        flops=2 * 6 * 2 * rows * width * half,
    )[0]


def terms_back_kernel(core, *refs):
    xs, (dq, dk, dv, wq, wk, wv, own, par, far, far_par, sums) = refs[:4], refs[4:]
    rows, width = xs[0].shape
    near = 2 * rows
    chip = trans_right(dk[:near], wk[...]) + trans_right(dv[:near], wv[...]) + trans_right(dq[...], wq[...])
    away = trans_right(dk[near:], wk[...]) + trans_right(dv[near:], wv[...])
    parts = (chip[:rows], chip[rows:], away[:rows], away[rows:])
    own[...] = parts[0]
    par[...] = parts[1].astype(BF)
    far[...] = parts[2]
    far_par[...] = parts[3].astype(BF)
    gain = jnp.zeros((1, width), F32)
    for x, terms in zip(xs, parts):
        normed, _ = norm_forward(x[...].astype(F32))
        gain = gain + column_sum(terms * normed)
    bias = column_sum(chip) + column_sum(away)
    sums[...] = jnp.concatenate([gain, bias, jnp.zeros((6, width), F32)], axis=0).astype(BF)


def terms_back(core, xs, dq, dk, dv, wq, wk, wv):
    rows, width = xs[0].shape
    half = width // 2
    weight = by_core((width, half), 1)
    ins = (*xs, dq, dk, dv, wq, wk, wv)
    return call(
        terms_back_kernel,
        "terms_back",
        core,
        ins,
        [weight if x.shape == (width, width) else whole(*x.shape) for x in ins],
        [shape(F32, rows, width), shape(BF, rows, width)] * 2 + [shape(BF, 8, width)],
        VMEM["terms_back"],
        flops=2 * 5 * 2 * rows * width * half,
    )


def finish_feed_kernel(core, mine_down, other_down, mine_up, other_up, w_down, w_up):
    ours = pl.program_id(0) == core[0]
    w_down[...] = jnp.where(ours, mine_down[0], other_down[0]).astype(F32)
    w_up[...] = jnp.where(ours, mine_up[0], other_up[0]).T.astype(F32)


def finish_feed(core, mine, other):
    _, block, width = mine.shape
    hidden = 8 * block

    def needed(half, first):
        def index(h, i, core):
            side = core[0] if half == 0 else 1 - core[0]
            at = jnp.where(h == side, i, jnp.where(h < side, 0, 3))
            return first + at, 0, 0

        return pl.BlockSpec((1, block, width), index)

    return pl.pallas_call(
        finish_feed_kernel,
        grid_spec=pltpu.PrefetchScalarGridSpec(
            num_scalar_prefetch=1,
            grid=(2, 4),
            in_specs=[needed(0, 0), needed(1, 0), needed(0, 4), needed(1, 4)],
            out_specs=[
                pl.BlockSpec((block, width), lambda h, i, core: (4 * h + i, 0)),
                pl.BlockSpec((width, block), lambda h, i, core: (0, 4 * h + i)),
            ],
        ),
        out_shape=[shape(F32, hidden, width), shape(F32, width, hidden)],
        compiler_params=params(VMEM["finish_feed"]),
        cost_estimate=pl.CostEstimate(flops=0, bytes_accessed=12 * hidden * width, transcendentals=0),
        name="finish_feed",
    )(core, mine, other, mine, other)


def finish_attend_kernel(core, mine, other, mine_vec, other_vec, wq, wk, wv, wo, *vecs):
    width = wq.shape[0]
    half = width // 2
    share = half // 2
    is_first = core[0] == 0
    for i, out in enumerate((wq, wk, wv, wo)):
        one, two = (
            jnp.concatenate([ref[2 * i, :share], ref[2 * i + 1, :share]], axis=0)
            for ref in (mine, other)
        )
        first = jnp.where(is_first, one, two)
        second = jnp.where(is_first, two, one)
        if i == 3:
            out[:half, :] = first.astype(F32)
            out[half:, :] = second.astype(F32)
        else:
            out[:, :half] = first.T.astype(F32)
            out[:, half:] = second.T.astype(F32)
    one, two = mine_vec[...].astype(F32), other_vec[...].astype(F32)
    both = one + two
    first = jnp.where(is_first, one, two)
    second = jnp.where(is_first, two, one)
    sums = sum(ref[i, share : share + 8].astype(F32) for ref in (mine, other) for i in range(8))
    for k in range(2):
        vecs[k][...] = sums[k]
    for k in range(4):
        vecs[2 + k][...] = both[k]
    up, query_bias, value_bias = vecs[6:]
    up[...] = jnp.concatenate([first[4], first[5], second[4], second[5]], axis=0)
    query_bias[...] = jnp.concatenate([first[6, :half], second[6, :half]], axis=0)
    value_bias[...] = jnp.concatenate([first[6, half:], second[6, half:]], axis=0)


def finish_attend(core, mine, other, mine_vec, other_vec, width, hidden):
    outs = [shape(F32, width, width)] * 4 + [shape(F32, width)] * 6
    outs += [shape(F32, hidden), shape(F32, width), shape(F32, width)]
    ins = (mine, other, mine_vec, other_vec)
    return call(
        finish_attend_kernel,
        "finish_attend",
        core,
        ins,
        [whole(*x.shape) for x in ins],
        outs,
        VMEM["finish_attend"],
    )


def finish_tokens_kernel(core, x, own, got, far, hidden_grad, gain, out):
    normed, rscale = norm_forward(x[...].astype(F32))
    grad = own[...] + got[...].astype(F32) + far[...].astype(F32)
    out[...] = hidden_grad[...] + norm_back(grad * gain[...][None, :], normed, rscale)


def finish_tokens(core, x, own, got, far, hidden_grad, gain):
    rows, width = x.shape
    return call(
        finish_tokens_kernel,
        "finish_tokens",
        core,
        (x, own, got, far, hidden_grad, gain),
        [whole(rows, width)] * 5 + [whole(width)],
        [shape(F32, rows, width)],
        VMEM["finish_tokens"],
    )[0]


def exchange(values, groups):
    return lax.all_to_all(values, BOTH, split_axis=0, concat_axis=0, axis_index_groups=groups)


def neighbours(axis):
    pairs = []
    for device in range(128):
        x, y, z, core = place_of(device)
        at = [x, y, z]
        at[axis] = 3 - at[axis] if core == 0 else at[axis] ^ 1
        x, y, z = at
        pairs.append((device, (x * 8 + (z // 2) * 4 + y) * 4 + (z % 2) * 2 + core))
    return pairs


ACROSS = [neighbours(axis) for axis in range(3)]


def add_along(parts, axes):
    got = [lax.ppermute(p, BOTH, ACROSS[axis]) for p, axis in zip(parts, axes)]
    return [(p.astype(F32) + g.astype(F32)).astype(BF) for p, g in zip(parts, got)]


def add_up_kernel(core, got, out):
    out[...] = sum(got[i].astype(F32) for i in range(8)).astype(BF)


def add_up(core, got):
    _, rows, width = got.shape
    return call(
        add_up_kernel, "add_up", core, (got,), [whole(*got.shape)], [shape(BF, rows, width)], VMEM["add_up"]
    )[0]


def per_device(
    tokens,
    lengths,
    ln1_gain,
    ln1_bias,
    w_query,
    b_query,
    w_key,
    w_value,
    b_value,
    w_out,
    b_out,
    ln2_gain,
    ln2_bias,
    w_up,
    b_up,
    w_down,
    b_down,
    cotangent,
):
    _, rows, width = tokens.shape
    hidden = w_up.shape[1]
    band = lax.axis_index("band")
    core = lax.rem(band, 2).reshape(1)
    together = lax.optimization_barrier

    own = tokens.reshape(rows, width)
    grad_own = cotangent.reshape(rows, width)
    far = swap_z(own)
    par = swap_core(own)
    grad_par = swap_core(grad_own)

    ends = jnp.cumsum(lengths[0])
    place = jnp.arange(rows, dtype=jnp.int32)
    slices = [band, band ^ 1, band ^ 2, band ^ 3]
    at_all = jnp.concatenate([s * rows + place for s in slices])
    seg_all = jnp.sum((at_all[:, None] >= ends[None, :]).astype(jnp.int32), axis=1)
    lanes = jnp.arange(SEGS, dtype=jnp.int32)
    count = lengths.shape[1]
    mask_q = (seg_all[None, : 2 * rows] == lanes[:, None]).astype(BF)
    mask_k = jnp.where(
        (seg_all[:, None] != lanes[None, :]) & (lanes[None, :] < count), -BARRED, 0.0
    ).astype(BF)

    params = (ln1_gain, ln1_bias, w_query, b_query, w_key, w_value, b_value)
    *near, q0, q1, part, stats = attend(core, (own, par), params, (mask_q, mask_k[: 2 * rows]))
    queries, before = (q0, q1), (part, stats)
    far, before, grad_par = together((far, before, grad_par))
    far_par = swap_core(far)
    *away, mix_own, mix_par, lse = attend(
        core, (far, far_par), params, (mask_q, mask_k[2 * rows :]), queries, before
    )
    attn, keys, values = ((near[i], near[3 + i], away[i], away[3 + i]) for i in range(3))
    mix_other = swap_core(mix_par)
    hidden1, mlp_own = middle(core, own, mix_own, mix_other, w_out, b_out, ln2_gain, ln2_bias)
    mlp_par = swap_core(mlp_own)
    sides = (mlp_own, mlp_par, grad_own, grad_par)
    act, gpre, db_up, dc_own, dc_par = feed(core, *sides, w_up, b_up, w_down)
    dc_got = swap_core(dc_par)
    group_1 = feed_weights(core, *sides, act, gpre)
    dc_got, group_1 = together((dc_got, group_1))
    dc_got = in_hbm(dc_got)
    grad_hidden1, grad_attn, sums_2 = middle_back(core, hidden1, dc_own, dc_got, grad_own, ln2_gain)
    grads = (grad_attn, swap_core(grad_attn))
    grads, group_1 = together((grads, group_1))
    mixed = (mix_own, mix_par)
    got_1 = exchange(group_1.reshape(8, -1, width), GROUPS_1)
    dq, dk, dv = attend_back(
        core, queries, keys, values, mask_q, mask_k, mixed, grads, w_out, lse
    )
    group_2 = weights_back(core, attn, dq, dk, dv, mixed, grads, sums_2, db_up)
    got_1, group_2 = together((got_1, group_2))
    got_2 = exchange(group_2, GROUPS_1)
    part_1 = add_up(core, got_1)
    part_1, dq = together((part_1, dq))
    (part_1,) = add_along([part_1], (0,))
    t_own, t_par, t_far, t_far_par, sums_1 = terms_back(
        core, (own, par, far, far_par), dq, dk, dv, w_query, w_key, w_value
    )
    part_1, t_par, t_far_par = together((part_1, t_par, t_far_par))
    (part_1,) = add_along([part_1], (1,))
    got_far, got_own = swap_core(t_far_par), swap_core(t_par)
    far_sum = (t_far + got_far.astype(F32)).astype(BF)
    part_1, got_2, far_sum = together((part_1, got_2, far_sum))
    part_2 = add_up(core, got_2)
    share = width // 4
    rest = jnp.concatenate([part_2[: share + VECTORS - 2], sums_1[:2]], axis=0)
    far_terms = swap_z(far_sum)
    part_1, rest = add_along([part_1, rest], (2, 0))

    def spread(values):
        return exchange(jnp.broadcast_to(values[None], (8,) + values.shape), GROUPS_1)

    total_1 = spread(part_1)
    (rest,) = add_along([rest], (1,))
    (rest,) = add_along([rest], (2,))
    act, _ = together((act, part_1))
    out_own, out_par = feed_out(core, act, w_down)
    layer_out = (hidden1 + out_own + swap_core(out_par).astype(F32) + b_down).astype(BF)
    rest, far_terms = together((rest, far_terms))
    grad_tokens = finish_tokens(core, own, t_own, got_own, far_terms, grad_hidden1, ln1_gain)
    total_1, rest, layer_out = together((total_1, rest, layer_out))
    vectors = rest[share:]
    total_2 = spread(jnp.concatenate([rest[:share], vectors[-2:], vectors[:6]], axis=0))
    other_1 = swap_core(total_1)
    other_vectors = swap_core(vectors)
    full_down, full_up = finish_feed(core, total_1, other_1)
    total_2, full_down, other_vectors, grad_tokens = together(
        (total_2, full_down, other_vectors, grad_tokens)
    )
    other_2 = swap_core(total_2)
    finished = finish_attend(core, total_2, other_2, vectors, other_vectors, width, hidden)
    full_query, full_key, full_value, full_out = finished[:4]
    d_gain1, d_bias1, d_gain2, d_bias2, d_b_out, d_b_down, d_b_up, d_b_query, d_b_value = finished[4:]
    return (
        layer_out[None],
        grad_tokens[None],
        d_gain1,
        d_bias1,
        full_query,
        d_b_query,
        full_key,
        full_value,
        d_b_value,
        full_out,
        d_b_out,
        d_gain2,
        d_bias2,
        full_up,
        d_b_up,
        full_down,
        d_b_down,
    )


def solution(mesh):
    split = P("dp", "band", None)
    return jax.shard_map(
        per_device,
        mesh=mesh,
        in_specs=(split, P("dp", None)) + (P(),) * 15 + (split,),
        out_specs=(split, split) + (P(),) * 15,
        check_vma=False,
    )
```

```python
import functools

import jax
import jax.numpy as jnp
from jax import lax
from jax.experimental import pallas as pl
from jax.experimental.pallas import tpu as pltpu
from jax.sharding import PartitionSpec as P

HEADS = 12
HDIM = 64
PAIR = 2 * HDIM
SEGS = 128
BARRED = 2.0**100
BF = jnp.bfloat16
F32 = jnp.float32
BOTH = ("dp", "band")
CORE = [(0, 1), (1, 0), (2, 3), (3, 2)]
ZLO = [(0, 2), (1, 3), (2, 0), (3, 1)]
BIT_A = (0, 1, 1, 0)
BIT_B = (0, 0, 1, 1)
ONCE = pl.Buffered(1)
VMEM = {
    "near": 34,
    "far": 28,
    "attend_back": 56,
    "middle": 14,
    "feed": 32,
    "feed_weights": 30,
    "feed_out": 30,
    "add_up": 24,
    "middle_back": 16,
    "weights_back": 56,
    "terms_back": 56,
    "finish_feed": 24,
    "finish_attend": 28,
    "finish_tokens": 56,
}


def place_of(device):
    dp, band = divmod(device, 4)
    x, rest = divmod(dp, 8)
    z_hi, y = divmod(rest, 4)
    z_lo, core = divmod(band, 2)
    return x, y, z_hi * 2 + z_lo, core


def cube_groups(first):
    groups = {}
    for device in range(128):
        x, y, z, core = place_of(device)
        fixed, moving = (BIT_B, BIT_A) if (core == 0) == first else (BIT_A, BIT_B)
        members = groups.setdefault((core, fixed[x], fixed[y], fixed[z]), [])
        members.append(((moving[x], moving[y], moving[z]), device))
    return [[device for _, device in sorted(members)] for members in groups.values()]


GROUPS_1 = cube_groups(True)


def matmul(left, right):
    return jnp.dot(left, right, preferred_element_type=F32)


def trans_left(left, right):
    return lax.dot_general(left, right, (((0,), (0,)), ((), ())), preferred_element_type=F32)


def trans_right(left, right):
    return lax.dot_general(left, right, (((1,), (1,)), ((), ())), preferred_element_type=F32)


def swap_core(values):
    return lax.ppermute(values, "band", CORE)


def swap_z(values):
    return lax.ppermute(values, "band", ZLO)


def norm_forward(values):
    centre = values - jnp.mean(values, axis=-1, keepdims=True)
    rscale = lax.rsqrt(jnp.mean(centre * centre, axis=-1, keepdims=True) + 1e-06)
    return centre * rscale, rscale


def norm_back(grad_norm, normed, rscale):
    first = jnp.mean(grad_norm, axis=-1, keepdims=True)
    second = jnp.mean(grad_norm * normed, axis=-1, keepdims=True)
    return rscale * (grad_norm - first - normed * second)


def column_sum(values):
    return jnp.sum(values, axis=0, keepdims=True)


def shape(dtype, *dims):
    return jax.ShapeDtypeStruct(dims, dtype)


def params(mebibytes):
    return pltpu.CompilerParams(vmem_limit_bytes=mebibytes * 2**20)


def whole(*dims):
    return pl.BlockSpec(dims, lambda i, core: (0,) * len(dims), pipeline_mode=ONCE)


def by_core(dims, axis):
    return pl.BlockSpec(
        dims,
        lambda i, core: tuple(core[0] if k == axis else 0 for k in range(len(dims))),
        pipeline_mode=ONCE,
    )


class Outgoing:
    def __init__(self, target, held, sem):
        self.target, self.held, self.sem, self.shape, self.copy = target, held, sem, held.shape, None

    def __setitem__(self, index, values):
        self.held[index] = values

    def __getitem__(self, index):
        return self.held[index]

    def send(self):
        self.copy = pltpu.make_async_copy(self.held, self.target, self.sem)
        self.copy.start()


def call(kernel, name, core, ins, in_specs, outs, vmem, scratch=(), flops=0, sent=(), pinned=()):
    first = len(ins)

    def body(core_ref, *refs):
        refs = list(refs)
        count = first + len(outs)
        held, sems = refs[count : count + len(sent)], refs[count + len(sent)] if sent else None
        own = refs[count + len(sent) + (1 if sent else 0) :]
        for k, i in enumerate(sent):
            refs[first + i] = Outgoing(refs[first + i], held[k], sems.at[k])
        kernel(core_ref, *refs[:count], *own)
        for i in sent:
            if refs[first + i].copy is None:
                refs[first + i].send()
        for i in sent:
            refs[first + i].copy.wait()

    holders = [pltpu.VMEM(outs[i].shape, outs[i].dtype) for i in sent]
    if sent:
        holders.append(pltpu.SemaphoreType.DMA((len(sent),)))
    traffic = sum(x.size * x.dtype.itemsize for x in list(ins) + list(outs))
    return pl.pallas_call(
        body,
        grid_spec=pltpu.PrefetchScalarGridSpec(
            num_scalar_prefetch=1,
            grid=(1,),
            in_specs=in_specs,
            out_specs=[
                pl.BlockSpec(memory_space=pltpu.HBM) if i in sent else whole(*x.shape)
                for i, x in enumerate(outs)
            ],
            scratch_shapes=holders + list(scratch),
        ),
        out_shape=[
            pltpu.HBM(x.shape, x.dtype) if i in sent or i in pinned else x for i, x in enumerate(outs)
        ],
        compiler_params=params(vmem),
        cost_estimate=pl.CostEstimate(flops=flops, bytes_accessed=traffic, transcendentals=0),
        name=name,
    )(core, *ins)


def in_hbm(values):
    return pltpu.with_memory_space_constraint(values, pltpu.HBM)


def core_half(core, vector):
    size = vector.shape[0] // 2
    values = vector[...]
    return jnp.where(core[0] == 0, values[:size], values[size:])[None, :]


def project_body(core, xs, weights, outs, with_query):
    gain, bias, wq, bq, wk, wv, bv = weights
    rows = xs[0].shape[0]
    for i, x in enumerate(xs):
        a_ref, k_ref, v_ref = outs[3 * i : 3 * i + 3]
        normed, _ = norm_forward(x[...].astype(F32))
        attn_in = (normed * gain[...][None, :] + bias[...][None, :]).astype(BF)
        a_ref[...] = attn_in
        k_ref[...] = matmul(attn_in, wk[...]).astype(BF)
        v_ref[...] = (matmul(attn_in, wv[...]) + core_half(core, bv)).astype(BF)
        if with_query:
            q_ref = outs[6 + i]
            q_ref[...] = (matmul(attn_in, wq[...]) + core_half(core, bq)).astype(BF) * 0.125


def head_rows(head, dims):
    return lax.broadcasted_iota(jnp.int32, dims, 0) // HDIM == head


def head_lanes(head, dims):
    return lax.broadcasted_iota(jnp.int32, dims, 1) // HDIM == head


KEY_BLOCK = 256
MAX_ROWS = 32


def attend_body(first, queries, keys, values, masks, before, outs, scratch):
    (q0, q1), (k0, k1), (v0, v1), (mq_ref, mk_ref) = queries, keys, values, masks
    s_buf, p_buf, rhs, vt, kx = scratch
    if first:
        o_ref, stat_ref = outs
    else:
        (o_ref, stat_ref), (mix0, mix1, lse_ref) = before, outs
    near, width = k0.shape
    rows_q = q0.shape[0]
    nq = 2 * rows_q
    nk = 2 * near
    heads = width // HDIM
    blocks = nk // KEY_BLOCK

    def prepare(head):
        pair = slice((head // 2) * PAIR, (head // 2 + 1) * PAIR)
        if head % 2 == 0:
            vt[(head // 2) % 2, :PAIR, :near] = v0[:, pair].T
            vt[(head // 2) % 2, :PAIR, near:] = v1[:, pair].T
            kx[(head // 2) % 2, :near, :PAIR] = k0[:, pair]
            kx[(head // 2) % 2, near:, :PAIR] = k1[:, pair]
        for at, ref in ((0, q0), (rows_q, q1)):
            turned = ref[:, pair].T
            rhs[head % 2, :PAIR, at : at + rows_q] = jnp.where(
                head_rows(head % 2, turned.shape), turned, jnp.zeros((), BF)
            )

    for i in range(2):
        vt[i, PAIR:] = jnp.ones((16, nk), BF)
        rhs[i, PAIR:] = mq_ref[...]
        kx[i, :, PAIR:] = mk_ref[...]
    peaks, outs, logs, norms = {}, [], [], []
    for t in range(heads + 2):
        if t < heads:
            prepare(t)
        peak, total = None, None
        for i in range(blocks):
            rows = slice(i * KEY_BLOCK, (i + 1) * KEY_BLOCK)
            if t < heads:
                scores = matmul(kx[(t // 2) % 2, rows, :], rhs[t % 2])
                s_buf[t % 2, rows, :] = scores
                for j in range(KEY_BLOCK // MAX_ROWS):
                    part = scores[j * MAX_ROWS : (j + 1) * MAX_ROWS]
                    peak = part if peak is None else jnp.maximum(peak, part)
            if 0 <= t - 1 < heads:
                p_buf[(t - 1) % 2, rows, :] = jnp.exp(
                    s_buf[(t - 1) % 2, rows, :] - peaks[t - 1]
                ).astype(BF)
            if 0 <= t - 2 < heads:
                part = matmul(vt[((t - 2) // 2) % 2, :, rows], p_buf[(t - 2) % 2, rows, :])
                total = part if total is None else total + part
        if t < heads:
            peaks[t] = jnp.max(peak, axis=0, keepdims=True)
            if not first:
                peaks[t] = jnp.maximum(peaks[t], stat_ref[t : t + 1, :])
        if 0 <= t - 2 < heads:
            head = t - 2
            side = head % 2
            own = slice(head * HDIM, (head + 1) * HDIM)
            norm = total[PAIR : PAIR + 1]
            mixed = total[side * HDIM : (side + 1) * HDIM]
            if first:
                o_ref[own, :] = mixed
                norms.append(norm)
                continue
            kept = jnp.exp(stat_ref[head : head + 1, :] - peaks[head])
            norm = norm + kept * stat_ref[8 + head : 9 + head, :]
            outs.append((mixed + kept * o_ref[own, :]) / norm)
            logs.append(peaks[head] + jnp.log(norm))
            if side == 1:
                pair = slice((head // 2) * PAIR, (head // 2 + 1) * PAIR)
                both = jnp.concatenate(outs[-2:], axis=0).T.astype(BF)
                mix0[:, pair] = both[:rows_q]
                mix1[:, pair] = both[rows_q:]
    spare = jnp.zeros((8 - heads, nq), F32)
    if first:
        stat_ref[...] = jnp.concatenate(
            [peaks[h] for h in range(heads)] + [spare] + norms + [spare], axis=0
        )
    else:
        for head in range(heads):
            lse_ref[head // 2, head % 2 : head % 2 + 1, :] = logs[head]


def near_kernel(core, *refs):
    xs, weights, masks = refs[:2], refs[2:9], refs[9:11]
    outs, tops, scratch = refs[11:19], refs[19:21], refs[21:]
    project_body(core, xs, weights, outs, True)
    for out in outs[:6]:
        out.send()
    a0, k0, v0, a1, k1, v1, q0, q1 = outs
    attend_body(True, (q0, q1), (k0, k1), (v0, v1), masks, None, tops, scratch)


def far_kernel(core, *refs):
    xs, weights, masks = refs[:2], refs[2:9], refs[9:11]
    queries, before, outs, tops, scratch = refs[11:13], refs[13:15], refs[15:21], refs[21:24], refs[24:]
    project_body(core, xs, weights, outs, False)
    for out in outs:
        out.send()
    a0, k0, v0, a1, k1, v1 = outs
    attend_body(False, queries, (k0, k1), (v0, v1), masks, before, tops, scratch)


def attend(core, xs, weights, masks, queries=(), before=()):
    rows, width = xs[0].shape
    half = width // 2
    heads = half // HDIM
    nq = nk = 2 * rows
    small = shape(BF, rows, half)
    outs = [shape(BF, rows, width), small, small] * 2
    if not before:
        outs += [small, small, shape(F32, half, nq), shape(F32, 16, nq)]
    else:
        outs += [small, small, shape(F32, heads // 2, 2, nq)]
    weight = by_core((width, half), 1)
    weights = [in_hbm(x) if x.ndim > 1 else x for x in weights]
    ins = (*xs, *weights, *masks, *queries, *before)
    return call(
        far_kernel if before else near_kernel,
        "attend",
        core,
        ins,
        [weight if x.shape == (width, width) else whole(*x.shape) for x in ins],
        outs,
        VMEM["far"] if before else VMEM["near"],
        [
            pltpu.VMEM((2, nk, nq), F32),
            pltpu.VMEM((2, nk, nq), BF),
            pltpu.VMEM((2, PAIR + SEGS, nq), BF),
            pltpu.VMEM((2, PAIR + 16, nk), BF),
            pltpu.VMEM((2, nk, PAIR + SEGS), BF),
        ],
        flops=2 * 2 * nq * nk * half * 4 + 2 * 2 * rows * width * half * 2,
        sent=tuple(range(6)) + ((8,) if before else ()),
    )


QUERY_BLOCK = 256


def attend_back_kernel(core, *refs):
    q0, q1, ks, vs = refs[0], refs[1], refs[2:6], refs[6:10]
    mq_ref, mk_ref, o0, o1, g0, g1, w_out, lse_ref, dq_ref, dk_ref, dv_ref, p_buf, ds_buf = refs[10:]
    nq = 2 * q0.shape[0]
    blocks = nq // QUERY_BLOCK
    nothing = jnp.zeros((), BF)
    upstream = jnp.concatenate([g0[...], g1[...]], axis=0)
    grad = trans_right(upstream, w_out[...]).astype(BF)
    query = jnp.concatenate([q0[...], q1[...]], axis=0)
    query_t, grad_t = query.T, grad.T
    key = jnp.concatenate([k[...] for k in ks], axis=0)
    value = jnp.concatenate([v[...] for v in vs], axis=0)
    key_t = key.T
    mixed = jnp.concatenate([o0[...], o1[...]], axis=0)
    product = grad_t.astype(F32) * mixed.T.astype(F32)
    key_masked = jnp.concatenate([key, mk_ref[...]], axis=1)
    mask_q = mq_ref[...]
    for b in range(blocks):
        cols = slice(b * QUERY_BLOCK, (b + 1) * QUERY_BLOCK)
        dqs = []
        for e in range(2):
            at = (e * blocks + b) * QUERY_BLOCK
            rows = head_rows(e, (PAIR, QUERY_BLOCK))
            query_e = jnp.where(rows, query_t[:, cols], nothing)
            grad_e = jnp.where(rows, grad_t[:, cols], nothing)
            scores = matmul(key_masked, jnp.concatenate([query_e, mask_q[:, cols]], axis=0))
            probs = jnp.exp(scores - lse_ref[0, e : e + 1, cols])
            p_buf[:, at : at + QUERY_BLOCK] = probs.astype(BF)
            grad_probs = matmul(value, grad_e)
            inner = jnp.sum(product[e * HDIM : (e + 1) * HDIM, cols], axis=0, keepdims=True)
            grad_scores = (probs * (grad_probs - inner)).astype(BF)
            ds_buf[:, at : at + QUERY_BLOCK] = grad_scores
            dqs.append(matmul(key_t, grad_scores)[e * HDIM : (e + 1) * HDIM])
        dq_ref[cols, :] = (jnp.concatenate(dqs, axis=0) * 0.125).T.astype(BF)

    def by_head(values):
        return jnp.concatenate(
            [jnp.where(head_lanes(e, values.shape), values, nothing) for e in range(2)], axis=0
        )

    dv_ref[...] = matmul(p_buf[...], by_head(grad)).astype(BF)
    dk_ref[...] = matmul(ds_buf[...], by_head(query)).astype(BF)


def attend_back(core, queries, keys, values, mask_q, mask_k, mixed, grads, w_out, lse):
    rows, width = queries[0].shape
    pairs = width // PAIR
    nq = 2 * rows
    nk = mask_k.shape[0]
    pair = lambda size: pl.BlockSpec((size, PAIR), lambda i, core: (0, i))
    outs = [shape(BF, size, width) for size in (nq, nk, nk)]
    ins = (*queries, *keys, *values, mask_q, mask_k, *mixed, *grads, w_out, lse)
    return pl.pallas_call(
        attend_back_kernel,
        grid_spec=pltpu.PrefetchScalarGridSpec(
            num_scalar_prefetch=1,
            grid=(pairs,),
            in_specs=[pair(rows)] * 10
            + [whole(SEGS, nq), whole(nk, SEGS)]
            + [pair(rows)] * 2
            + [whole(rows, 2 * width)] * 2
            + [pl.BlockSpec((PAIR, 2 * width), lambda i, core: (core[0] * pairs + i, 0))]
            + [pl.BlockSpec((1, 2, nq), lambda i, core: (i, 0, 0))],
            out_specs=[pair(nq), pair(nk), pair(nk)],
            scratch_shapes=[pltpu.VMEM((nk, 2 * nq), BF)] * 2,
        ),
        out_shape=outs,
        compiler_params=params(VMEM["attend_back"]),
        cost_estimate=pl.CostEstimate(
            flops=2 * 5 * nq * nk * width * 4,
            bytes_accessed=sum(x.size * x.dtype.itemsize for x in ins + tuple(outs)),
            transcendentals=0,
        ),
        name="attend_back",
    )(core, *ins)


def middle_kernel(core, x_ref, mine, other, w_out, b_out, gain, bias, h_ref, c_ref):
    half = mine.shape[1]
    at = pl.multiple_of(core[0] * half, 128)
    away = pl.multiple_of((1 - core[0]) * half, 128)
    hidden1 = x_ref[...].astype(F32) + (
        matmul(mine[...], w_out[pl.ds(at, half), :])
        + matmul(other[...], w_out[pl.ds(away, half), :])
        + b_out[...][None, :]
    )
    h_ref[...] = hidden1
    normed, _ = norm_forward(hidden1)
    c_ref[...] = (normed * gain[...][None, :] + bias[...][None, :]).astype(BF)


def middle(core, x, mine, other, w_out, b_out, gain, bias):
    rows, width = x.shape
    half = width // 2
    return call(
        middle_kernel,
        "middle",
        core,
        (x, mine, other, w_out, b_out, gain, bias),
        [whole(rows, width), whole(rows, half), whole(rows, half), whole(width, width)]
        + [whole(width)] * 3,
        [shape(F32, rows, width), shape(BF, rows, width)],
        VMEM["middle"],
        flops=2 * rows * width * width,
    )


HIDDEN_BLOCK = 512


def gelu_parts(values):
    bell = jnp.exp(values * values * -0.5)
    k = 1.0 / (1.0 + 0.23164188838 * jnp.abs(values))
    tail = 0.7107068705 + k * (-0.7265760135 + k * 0.5307027145)
    tail = k * (0.127414796 + k * (-0.142248368 + k * tail)) * bell
    below = jnp.where(values >= 0, 1.0 - tail, tail)
    return values * below, below + values * bell * 0.3989422804014327


def feed_kernel(core, c0, c1, g0, g1, w_up, b_up, w_down, act, gpre, db_up, dc0, dc1, pre, dact):
    rows = c0.shape[0]
    normed = jnp.concatenate([c0[...], c1[...]], axis=0)
    grad = jnp.concatenate([g0[...], g1[...]], axis=0)
    steps = w_up.shape[1] // HIDDEN_BLOCK
    bias = core_half(core, b_up)
    for t in range(steps + 1):
        if t < steps:
            part = slice(t * HIDDEN_BLOCK, (t + 1) * HIDDEN_BLOCK)
            pre[t % 2] = matmul(normed, w_up[:, part])
            dact[t % 2] = trans_right(grad, w_down[part, :])
        if t > 0:
            part = slice((t - 1) * HIDDEN_BLOCK, t * HIDDEN_BLOCK)
            value, slope = gelu_parts(pre[(t - 1) % 2] + bias[:, part])
            low = (dact[(t - 1) % 2] * slope).astype(BF)
            act[:, part] = value.astype(BF)
            gpre[:, part] = low
            db_up[:, part] = column_sum(low.astype(F32))
    grad_in = trans_right(gpre[...], w_up[...])
    dc0[...] = grad_in[:rows]
    dc1[...] = grad_in[rows:].astype(BF)


def feed(core, c0, c1, g0, g1, w_up, b_up, w_down):
    rows, width = c0.shape
    half = w_up.shape[1] // 2
    return call(
        feed_kernel,
        "feed",
        core,
        (c0, c1, g0, g1, w_up, b_up, w_down),
        [whole(rows, width)] * 4
        + [by_core((width, half), 1), whole(2 * half), by_core((half, width), 0)],
        [shape(BF, 2 * rows, half)] * 2
        + [shape(F32, 1, half), shape(F32, rows, width), shape(BF, rows, width)],
        VMEM["feed"],
        [pltpu.VMEM((2, 2 * rows, HIDDEN_BLOCK), F32)] * 2,
        pinned=(2,),
        flops=2 * 3 * 2 * rows * width * half,
    )


def feed_weights_kernel(core, c0, c1, g0, g1, act, gpre, dw_out, dw, sems):
    normed = jnp.concatenate([c0[...], c1[...]], axis=0)
    grad = jnp.concatenate([g0[...], g1[...]], axis=0)
    hidden = act.shape[1]
    copies = []
    for t in range(hidden // HIDDEN_BLOCK):
        part = slice(t * HIDDEN_BLOCK, (t + 1) * HIDDEN_BLOCK)
        turned = slice(hidden + t * HIDDEN_BLOCK, hidden + (t + 1) * HIDDEN_BLOCK)
        dw[part, :] = trans_left(act[:, part], grad).astype(BF)
        dw[turned, :] = trans_left(gpre[:, part], normed).astype(BF)
        for k, span in enumerate((part, turned)):
            copies.append(
                pltpu.make_async_copy(dw.at[span, :], dw_out.at[span, :], sems.at[2 * t + k])
            )
            copies[-1].start()
    for copy in copies:
        copy.wait()


def feed_weights(core, c0, c1, g0, g1, act, gpre):
    rows, width = c0.shape
    half = act.shape[1]
    ins = (c0, c1, g0, g1, act, gpre)
    return pl.pallas_call(
        feed_weights_kernel,
        grid_spec=pltpu.PrefetchScalarGridSpec(
            num_scalar_prefetch=1,
            grid=(1,),
            in_specs=[whole(*x.shape) for x in ins],
            out_specs=pl.BlockSpec(memory_space=pltpu.HBM),
            scratch_shapes=[
                pltpu.VMEM((2 * half, width), BF),
                pltpu.SemaphoreType.DMA((2 * half // HIDDEN_BLOCK,)),
            ],
        ),
        out_shape=pltpu.HBM((2 * half, width), BF),
        compiler_params=params(VMEM["feed_weights"]),
        cost_estimate=pl.CostEstimate(
            flops=2 * 2 * 2 * rows * width * half,
            bytes_accessed=2 * (4 * rows * width + 4 * rows * half + 2 * half * width),
            transcendentals=0,
        ),
        name="feed_weights",
    )(core, *ins)


def feed_out_kernel(core, act, w_down, out0, out1):
    rows = out0.shape[0]
    out = matmul(act[...], w_down[...])
    out0[...] = out[:rows]
    out1[...] = out[rows:].astype(BF)


def feed_out(core, act, w_down):
    rows, half = act.shape[0] // 2, act.shape[1]
    width = w_down.shape[1]
    return call(
        feed_out_kernel,
        "feed_out",
        core,
        (act, w_down),
        [whole(2 * rows, half), by_core((half, width), 0)],
        [shape(F32, rows, width), shape(BF, rows, width)],
        VMEM["feed_out"],
        flops=2 * 2 * rows * width * half,
    )


def middle_back_kernel(core, h_ref, own, got, g_ref, gain, out, low, sums):
    normed, rscale = norm_forward(h_ref[...])
    grad_in = own[...] + got[...].astype(F32)
    upstream = g_ref[...].astype(F32)
    grad = upstream + norm_back(grad_in * gain[...][None, :], normed, rscale)
    out[...] = grad
    rounded = grad.astype(BF)
    low[...] = rounded
    sums[...] = jnp.concatenate(
        [
            column_sum(grad_in * normed),
            column_sum(grad_in),
            column_sum(rounded.astype(F32)),
            column_sum(upstream),
            jnp.zeros((4, sums.shape[1]), F32),
        ],
        axis=0,
    )


def middle_back(core, hidden1, own, got, grad, gain):
    rows, width = hidden1.shape
    return call(
        middle_back_kernel,
        "middle_back",
        core,
        (hidden1, own, got, grad, gain),
        [whole(rows, width)] * 4 + [whole(width)],
        [shape(F32, rows, width), shape(BF, rows, width), shape(F32, 8, width)],
        VMEM["middle_back"],
        pinned=(0, 2),
    )


VECTORS = 16


def weights_back_kernel(core, *refs):
    attn, (dq, dk, dv, mix0, mix1, g0, g1, sums_2, db_up, grads) = refs[:4], refs[4:]
    rows, width = attn[0].shape
    half = width // 2
    a_near = jnp.concatenate([attn[0][...], attn[1][...]], axis=0)
    a_all = jnp.concatenate([a_near, attn[2][...], attn[3][...]], axis=0)
    mixed = jnp.concatenate([mix0[...], mix1[...]], axis=0)
    upstream = jnp.concatenate([g0[...], g1[...]], axis=0)
    stacked = [
        trans_left(dq[...], a_near),
        trans_left(dk[...], a_all),
        trans_left(dv[...], a_all),
        trans_left(mixed, upstream),
    ]
    share = half // 2
    for i, block in enumerate(stacked):
        low = block.astype(BF)
        grads[2 * i, :share, :] = low[:share]
        grads[2 * i + 1, :share, :] = low[share:]
    halves = jnp.concatenate(
        [column_sum(dq[...].astype(F32)), column_sum(dv[...].astype(F32))], axis=1
    )
    vectors = jnp.concatenate(
        [sums_2[0:4, :], db_up[:, :width], db_up[:, width:], halves]
        + [jnp.zeros((VECTORS - 7, width), F32)],
        axis=0,
    ).astype(BF)
    for i in range(8):
        grads[i, share:, :] = vectors


def weights_back(core, attn, dq, dk, dv, mixed, grads, sums_2, db_up):
    rows, width = attn[0].shape
    half = width // 2
    ins = (*attn, dq, dk, dv, *mixed, *grads, sums_2, db_up)
    return call(
        weights_back_kernel,
        "weights_back",
        core,
        ins,
        [whole(*x.shape) for x in ins],
        [shape(BF, 8, width // 4 + VECTORS, width)],
        VMEM["weights_back"],
        flops=2 * 6 * 2 * rows * width * half,
    )[0]


def terms_back_kernel(core, *refs):
    xs, (dq, dk, dv, wq, wk, wv, own, par, far, far_par, sums) = refs[:4], refs[4:]
    rows, width = xs[0].shape
    near = 2 * rows
    chip = trans_right(dk[:near], wk[...]) + trans_right(dv[:near], wv[...]) + trans_right(dq[...], wq[...])
    away = trans_right(dk[near:], wk[...]) + trans_right(dv[near:], wv[...])
    parts = (chip[:rows], chip[rows:], away[:rows], away[rows:])
    own[...] = parts[0]
    par[...] = parts[1].astype(BF)
    far[...] = parts[2]
    far_par[...] = parts[3].astype(BF)
    gain = jnp.zeros((1, width), F32)
    for x, terms in zip(xs, parts):
        normed, _ = norm_forward(x[...].astype(F32))
        gain = gain + column_sum(terms * normed)
    bias = column_sum(chip) + column_sum(away)
    sums[...] = jnp.concatenate([gain, bias, jnp.zeros((6, width), F32)], axis=0).astype(BF)


def terms_back(core, xs, dq, dk, dv, wq, wk, wv):
    rows, width = xs[0].shape
    half = width // 2
    weight = by_core((width, half), 1)
    ins = (*xs, dq, dk, dv, wq, wk, wv)
    return call(
        terms_back_kernel,
        "terms_back",
        core,
        ins,
        [weight if x.shape == (width, width) else whole(*x.shape) for x in ins],
        [shape(F32, rows, width), shape(BF, rows, width)] * 2 + [shape(BF, 8, width)],
        VMEM["terms_back"],
        flops=2 * 5 * 2 * rows * width * half,
    )


def finish_feed_kernel(core, mine_down, other_down, mine_up, other_up, w_down, w_up):
    ours = pl.program_id(0) == core[0]
    w_down[...] = jnp.where(ours, mine_down[0], other_down[0]).astype(F32)
    w_up[...] = jnp.where(ours, mine_up[0], other_up[0]).T.astype(F32)


def finish_feed(core, mine, other):
    _, block, width = mine.shape
    hidden = 8 * block

    def needed(half, first):
        def index(h, i, core):
            side = core[0] if half == 0 else 1 - core[0]
            at = jnp.where(h == side, i, jnp.where(h < side, 0, 3))
            return first + at, 0, 0

        return pl.BlockSpec((1, block, width), index)

    return pl.pallas_call(
        finish_feed_kernel,
        grid_spec=pltpu.PrefetchScalarGridSpec(
            num_scalar_prefetch=1,
            grid=(2, 4),
            in_specs=[needed(0, 0), needed(1, 0), needed(0, 4), needed(1, 4)],
            out_specs=[
                pl.BlockSpec((block, width), lambda h, i, core: (4 * h + i, 0)),
                pl.BlockSpec((width, block), lambda h, i, core: (0, 4 * h + i)),
            ],
        ),
        out_shape=[shape(F32, hidden, width), shape(F32, width, hidden)],
        compiler_params=params(VMEM["finish_feed"]),
        cost_estimate=pl.CostEstimate(flops=0, bytes_accessed=12 * hidden * width, transcendentals=0),
        name="finish_feed",
    )(core, mine, other, mine, other)


def finish_attend_kernel(core, mine, other, mine_vec, other_vec, wq, wk, wv, wo, *vecs):
    width = wq.shape[0]
    half = width // 2
    share = half // 2
    is_first = core[0] == 0
    for i, out in enumerate((wq, wk, wv, wo)):
        one, two = (
            jnp.concatenate([ref[2 * i, :share], ref[2 * i + 1, :share]], axis=0)
            for ref in (mine, other)
        )
        first = jnp.where(is_first, one, two)
        second = jnp.where(is_first, two, one)
        if i == 3:
            out[:half, :] = first.astype(F32)
            out[half:, :] = second.astype(F32)
        else:
            out[:, :half] = first.T.astype(F32)
            out[:, half:] = second.T.astype(F32)
    one, two = mine_vec[...].astype(F32), other_vec[...].astype(F32)
    both = one + two
    first = jnp.where(is_first, one, two)
    second = jnp.where(is_first, two, one)
    sums = sum(ref[i, share : share + 8].astype(F32) for ref in (mine, other) for i in range(8))
    for k in range(2):
        vecs[k][...] = sums[k]
    for k in range(4):
        vecs[2 + k][...] = both[k]
    up, query_bias, value_bias = vecs[6:]
    up[...] = jnp.concatenate([first[4], first[5], second[4], second[5]], axis=0)
    query_bias[...] = jnp.concatenate([first[6, :half], second[6, :half]], axis=0)
    value_bias[...] = jnp.concatenate([first[6, half:], second[6, half:]], axis=0)


def finish_attend(core, mine, other, mine_vec, other_vec, width, hidden):
    outs = [shape(F32, width, width)] * 4 + [shape(F32, width)] * 6
    outs += [shape(F32, hidden), shape(F32, width), shape(F32, width)]
    ins = (mine, other, mine_vec, other_vec)
    return call(
        finish_attend_kernel,
        "finish_attend",
        core,
        ins,
        [whole(*x.shape) for x in ins],
        outs,
        VMEM["finish_attend"],
    )


def finish_tokens_kernel(core, x, own, got, far, hidden_grad, gain, out):
    normed, rscale = norm_forward(x[...].astype(F32))
    grad = own[...] + got[...].astype(F32) + far[...].astype(F32)
    out[...] = hidden_grad[...] + norm_back(grad * gain[...][None, :], normed, rscale)


def finish_tokens(core, x, own, got, far, hidden_grad, gain):
    rows, width = x.shape
    return call(
        finish_tokens_kernel,
        "finish_tokens",
        core,
        (x, own, got, far, hidden_grad, gain),
        [whole(rows, width)] * 5 + [whole(width)],
        [shape(F32, rows, width)],
        VMEM["finish_tokens"],
    )[0]


def exchange(values, groups):
    return lax.all_to_all(values, BOTH, split_axis=0, concat_axis=0, axis_index_groups=groups)


def neighbours(axis):
    pairs = []
    for device in range(128):
        x, y, z, core = place_of(device)
        at = [x, y, z]
        at[axis] = 3 - at[axis] if core == 0 else at[axis] ^ 1
        x, y, z = at
        pairs.append((device, (x * 8 + (z // 2) * 4 + y) * 4 + (z % 2) * 2 + core))
    return pairs


ACROSS = [neighbours(axis) for axis in range(3)]


def add_along(parts, axes):
    got = [lax.ppermute(p, BOTH, ACROSS[axis]) for p, axis in zip(parts, axes)]
    return [(p.astype(F32) + g.astype(F32)).astype(BF) for p, g in zip(parts, got)]


def add_up_kernel(core, got, out):
    out[...] = sum(got[i].astype(F32) for i in range(8)).astype(BF)


def add_up(core, got):
    _, rows, width = got.shape
    return call(
        add_up_kernel, "add_up", core, (got,), [whole(*got.shape)], [shape(BF, rows, width)], VMEM["add_up"]
    )[0]


def per_device(
    tokens,
    lengths,
    ln1_gain,
    ln1_bias,
    w_query,
    b_query,
    w_key,
    w_value,
    b_value,
    w_out,
    b_out,
    ln2_gain,
    ln2_bias,
    w_up,
    b_up,
    w_down,
    b_down,
    cotangent,
):
    _, rows, width = tokens.shape
    hidden = w_up.shape[1]
    band = lax.axis_index("band")
    core = lax.rem(band, 2).reshape(1)
    together = lax.optimization_barrier

    own = tokens.reshape(rows, width)
    grad_own = cotangent.reshape(rows, width)
    far = swap_z(own)
    par = swap_core(own)
    grad_par = swap_core(grad_own)

    ends = jnp.cumsum(lengths[0])
    place = jnp.arange(rows, dtype=jnp.int32)
    slices = [band, band ^ 1, band ^ 2, band ^ 3]
    at_all = jnp.concatenate([s * rows + place for s in slices])
    seg_all = jnp.sum((at_all[:, None] >= ends[None, :]).astype(jnp.int32), axis=1)
    lanes = jnp.arange(SEGS, dtype=jnp.int32)
    count = lengths.shape[1]
    mask_q = (seg_all[None, : 2 * rows] == lanes[:, None]).astype(BF)
    mask_k = jnp.where(
        (seg_all[:, None] != lanes[None, :]) & (lanes[None, :] < count), -BARRED, 0.0
    ).astype(BF)

    params = (ln1_gain, ln1_bias, w_query, b_query, w_key, w_value, b_value)
    *near, q0, q1, part, stats = attend(core, (own, par), params, (mask_q, mask_k[: 2 * rows]))
    queries, before = (q0, q1), (part, stats)
    far, before, grad_par = together((far, before, grad_par))
    far_par = swap_core(far)
    *away, mix_own, mix_par, lse = attend(
        core, (far, far_par), params, (mask_q, mask_k[2 * rows :]), queries, before
    )
    attn, keys, values = ((near[i], near[3 + i], away[i], away[3 + i]) for i in range(3))
    mix_other = swap_core(mix_par)
    hidden1, mlp_own = middle(core, own, mix_own, mix_other, w_out, b_out, ln2_gain, ln2_bias)
    mlp_par = swap_core(mlp_own)
    sides = (mlp_own, mlp_par, grad_own, grad_par)
    act, gpre, db_up, dc_own, dc_par = feed(core, *sides, w_up, b_up, w_down)
    dc_got = swap_core(dc_par)
    group_1 = feed_weights(core, *sides, act, gpre)
    dc_got, group_1 = together((dc_got, group_1))
    dc_got = in_hbm(dc_got)
    grad_hidden1, grad_attn, sums_2 = middle_back(core, hidden1, dc_own, dc_got, grad_own, ln2_gain)
    grads = (grad_attn, swap_core(grad_attn))
    grads, group_1 = together((grads, group_1))
    mixed = (mix_own, mix_par)
    got_1 = exchange(group_1.reshape(8, -1, width), GROUPS_1)
    dq, dk, dv = attend_back(
        core, queries, keys, values, mask_q, mask_k, mixed, grads, w_out, lse
    )
    group_2 = weights_back(core, attn, dq, dk, dv, mixed, grads, sums_2, db_up)
    got_1, group_2 = together((got_1, group_2))
    got_2 = exchange(group_2, GROUPS_1)
    part_1 = add_up(core, got_1)
    part_1, dq = together((part_1, dq))
    (part_1,) = add_along([part_1], (0,))
    t_own, t_par, t_far, t_far_par, sums_1 = terms_back(
        core, (own, par, far, far_par), dq, dk, dv, w_query, w_key, w_value
    )
    part_1, t_par, t_far_par = together((part_1, t_par, t_far_par))
    (part_1,) = add_along([part_1], (1,))
    got_far, got_own = swap_core(t_far_par), swap_core(t_par)
    far_sum = (t_far + got_far.astype(F32)).astype(BF)
    part_1, got_2, far_sum, got_own = together((part_1, got_2, far_sum, got_own))
    part_2 = add_up(core, got_2)
    share = width // 4
    rest = jnp.concatenate([part_2[: share + VECTORS - 2], sums_1[:2]], axis=0)
    far_terms = swap_z(far_sum)
    part_1, rest = add_along([part_1, rest], (2, 0))
    part_1, rest = together((part_1, rest))

    def spread(values):
        return exchange(jnp.broadcast_to(values[None], (8,) + values.shape), GROUPS_1)

    total_1 = spread(part_1)
    (rest,) = add_along([rest], (1,))
    (rest,) = add_along([rest], (2,))
    act, _ = together((act, part_1))
    out_own, out_par = feed_out(core, act, w_down)
    layer_out = (hidden1 + out_own + swap_core(out_par).astype(F32) + b_down).astype(BF)
    total_1, rest, layer_out = together((total_1, rest, layer_out))
    vectors = rest[share:]
    total_2 = spread(jnp.concatenate([rest[:share], vectors[-2:], vectors[:6]], axis=0))
    total_1, far_terms = together((total_1, far_terms))
    other_1 = swap_core(total_1)
    other_vectors = swap_core(vectors)
    full_down, full_up = finish_feed(core, total_1, other_1)
    total_2, full_down, other_vectors, t_own = together(
        (total_2, full_down, other_vectors, t_own)
    )
    other_2 = swap_core(total_2)
    grad_tokens = finish_tokens(core, own, t_own, got_own, far_terms, grad_hidden1, ln1_gain)
    other_2, grad_tokens = together((other_2, grad_tokens))
    finished = finish_attend(core, total_2, other_2, vectors, other_vectors, width, hidden)
    full_query, full_key, full_value, full_out = finished[:4]
    d_gain1, d_bias1, d_gain2, d_bias2, d_b_out, d_b_down, d_b_up, d_b_query, d_b_value = finished[4:]
    return (
        layer_out[None],
        grad_tokens[None],
        d_gain1,
        d_bias1,
        full_query,
        d_b_query,
        full_key,
        full_value,
        d_b_value,
        full_out,
        d_b_out,
        d_gain2,
        d_bias2,
        full_up,
        d_b_up,
        full_down,
        d_b_down,
    )


def solution(mesh):
    split = P("dp", "band", None)
    return jax.shard_map(
        per_device,
        mesh=mesh,
        in_specs=(split, P("dp", None)) + (P(),) * 15 + (split,),
        out_specs=(split, split) + (P(),) * 15,
        check_vma=False,
    )
```

```python
import functools

import jax
import jax.numpy as jnp
from jax import lax
from jax.experimental import pallas as pl
from jax.experimental.pallas import tpu as pltpu
from jax.sharding import PartitionSpec as P

HEADS = 12
HDIM = 64
PAIR = 2 * HDIM
SEGS = 128
BARRED = 2.0**100
BF = jnp.bfloat16
F32 = jnp.float32
BOTH = ("dp", "band")
CORE = [(0, 1), (1, 0), (2, 3), (3, 2)]
ZLO = [(0, 2), (1, 3), (2, 0), (3, 1)]
BIT_A = (0, 1, 1, 0)
BIT_B = (0, 0, 1, 1)
ONCE = pl.Buffered(1)
VMEM = {
    "near": 34,
    "far": 28,
    "attend_back": 56,
    "middle": 14,
    "feed": 32,
    "feed_weights": 30,
    "feed_out": 30,
    "add_up": 24,
    "middle_back": 16,
    "weights_back": 56,
    "terms_back": 56,
    "finish_feed": 24,
    "finish_attend": 28,
    "finish_tokens": 56,
}


def place_of(device):
    dp, band = divmod(device, 4)
    x, rest = divmod(dp, 8)
    z_hi, y = divmod(rest, 4)
    z_lo, core = divmod(band, 2)
    return x, y, z_hi * 2 + z_lo, core


def cube_groups(first):
    groups = {}
    for device in range(128):
        x, y, z, core = place_of(device)
        fixed, moving = (BIT_B, BIT_A) if (core == 0) == first else (BIT_A, BIT_B)
        members = groups.setdefault((core, fixed[x], fixed[y], fixed[z]), [])
        members.append(((moving[x], moving[y], moving[z]), device))
    return [[device for _, device in sorted(members)] for members in groups.values()]


GROUPS_1 = cube_groups(True)


def matmul(left, right):
    return jnp.dot(left, right, preferred_element_type=F32)


def trans_left(left, right):
    return lax.dot_general(left, right, (((0,), (0,)), ((), ())), preferred_element_type=F32)


def trans_right(left, right):
    return lax.dot_general(left, right, (((1,), (1,)), ((), ())), preferred_element_type=F32)


def swap_core(values):
    return lax.ppermute(values, "band", CORE)


def swap_z(values):
    return lax.ppermute(values, "band", ZLO)


def norm_forward(values):
    centre = values - jnp.mean(values, axis=-1, keepdims=True)
    rscale = lax.rsqrt(jnp.mean(centre * centre, axis=-1, keepdims=True) + 1e-06)
    return centre * rscale, rscale


def norm_back(grad_norm, normed, rscale):
    first = jnp.mean(grad_norm, axis=-1, keepdims=True)
    second = jnp.mean(grad_norm * normed, axis=-1, keepdims=True)
    return rscale * (grad_norm - first - normed * second)


def column_sum(values):
    return jnp.sum(values, axis=0, keepdims=True)


def shape(dtype, *dims):
    return jax.ShapeDtypeStruct(dims, dtype)


def params(mebibytes):
    return pltpu.CompilerParams(vmem_limit_bytes=mebibytes * 2**20)


def whole(*dims):
    return pl.BlockSpec(dims, lambda i, core: (0,) * len(dims), pipeline_mode=ONCE)


def by_core(dims, axis):
    return pl.BlockSpec(
        dims,
        lambda i, core: tuple(core[0] if k == axis else 0 for k in range(len(dims))),
        pipeline_mode=ONCE,
    )


class Outgoing:
    def __init__(self, target, held, sem):
        self.target, self.held, self.sem, self.shape, self.copy = target, held, sem, held.shape, None

    def __setitem__(self, index, values):
        self.held[index] = values

    def __getitem__(self, index):
        return self.held[index]

    def send(self):
        self.copy = pltpu.make_async_copy(self.held, self.target, self.sem)
        self.copy.start()


def call(kernel, name, core, ins, in_specs, outs, vmem, scratch=(), flops=0, sent=(), pinned=()):
    first = len(ins)

    def body(core_ref, *refs):
        refs = list(refs)
        count = first + len(outs)
        held, sems = refs[count : count + len(sent)], refs[count + len(sent)] if sent else None
        own = refs[count + len(sent) + (1 if sent else 0) :]
        for k, i in enumerate(sent):
            refs[first + i] = Outgoing(refs[first + i], held[k], sems.at[k])
        kernel(core_ref, *refs[:count], *own)
        for i in sent:
            if refs[first + i].copy is None:
                refs[first + i].send()
        for i in sent:
            refs[first + i].copy.wait()

    holders = [pltpu.VMEM(outs[i].shape, outs[i].dtype) for i in sent]
    if sent:
        holders.append(pltpu.SemaphoreType.DMA((len(sent),)))
    traffic = sum(x.size * x.dtype.itemsize for x in list(ins) + list(outs))
    return pl.pallas_call(
        body,
        grid_spec=pltpu.PrefetchScalarGridSpec(
            num_scalar_prefetch=1,
            grid=(1,),
            in_specs=in_specs,
            out_specs=[
                pl.BlockSpec(memory_space=pltpu.HBM) if i in sent else whole(*x.shape)
                for i, x in enumerate(outs)
            ],
            scratch_shapes=holders + list(scratch),
        ),
        out_shape=[
            pltpu.HBM(x.shape, x.dtype) if i in sent or i in pinned else x for i, x in enumerate(outs)
        ],
        compiler_params=params(vmem),
        cost_estimate=pl.CostEstimate(flops=flops, bytes_accessed=traffic, transcendentals=0),
        name=name,
    )(core, *ins)


def in_hbm(values):
    return pltpu.with_memory_space_constraint(values, pltpu.HBM)


def core_half(core, vector):
    size = vector.shape[0] // 2
    values = vector[...]
    return jnp.where(core[0] == 0, values[:size], values[size:])[None, :]


def project_body(core, xs, weights, outs, with_query):
    gain, bias, wq, bq, wk, wv, bv = weights
    rows = xs[0].shape[0]
    for i, x in enumerate(xs):
        a_ref, k_ref, v_ref = outs[3 * i : 3 * i + 3]
        normed, _ = norm_forward(x[...].astype(F32))
        attn_in = (normed * gain[...][None, :] + bias[...][None, :]).astype(BF)
        a_ref[...] = attn_in
        k_ref[...] = matmul(attn_in, wk[...]).astype(BF)
        v_ref[...] = (matmul(attn_in, wv[...]) + core_half(core, bv)).astype(BF)
        if with_query:
            q_ref = outs[6 + i]
            q_ref[...] = (matmul(attn_in, wq[...]) + core_half(core, bq)).astype(BF) * 0.125


def head_rows(head, dims):
    return lax.broadcasted_iota(jnp.int32, dims, 0) // HDIM == head


def head_lanes(head, dims):
    return lax.broadcasted_iota(jnp.int32, dims, 1) // HDIM == head


KEY_BLOCK = 256
MAX_ROWS = 32


def attend_body(first, queries, keys, values, masks, before, outs, scratch):
    (q0, q1), (k0, k1), (v0, v1), (mq_ref, mk_ref) = queries, keys, values, masks
    s_buf, p_buf, rhs, vt, kx = scratch
    if first:
        o_ref, stat_ref = outs
    else:
        (o_ref, stat_ref), (mix0, mix1, lse_ref) = before, outs
    near, width = k0.shape
    rows_q = q0.shape[0]
    nq = 2 * rows_q
    nk = 2 * near
    heads = width // HDIM
    blocks = nk // KEY_BLOCK

    def prepare(head):
        pair = slice((head // 2) * PAIR, (head // 2 + 1) * PAIR)
        if head % 2 == 0:
            vt[(head // 2) % 2, :PAIR, :near] = v0[:, pair].T
            vt[(head // 2) % 2, :PAIR, near:] = v1[:, pair].T
            kx[(head // 2) % 2, :near, :PAIR] = k0[:, pair]
            kx[(head // 2) % 2, near:, :PAIR] = k1[:, pair]
        for at, ref in ((0, q0), (rows_q, q1)):
            turned = ref[:, pair].T
            rhs[head % 2, :PAIR, at : at + rows_q] = jnp.where(
                head_rows(head % 2, turned.shape), turned, jnp.zeros((), BF)
            )

    for i in range(2):
        vt[i, PAIR:] = jnp.ones((16, nk), BF)
        rhs[i, PAIR:] = mq_ref[...]
        kx[i, :, PAIR:] = mk_ref[...]
    peaks, outs, logs, norms = {}, [], [], []
    for t in range(heads + 2):
        if t < heads:
            prepare(t)
        peak, total = None, None
        for i in range(blocks):
            rows = slice(i * KEY_BLOCK, (i + 1) * KEY_BLOCK)
            if t < heads:
                scores = matmul(kx[(t // 2) % 2, rows, :], rhs[t % 2])
                s_buf[t % 2, rows, :] = scores
                for j in range(KEY_BLOCK // MAX_ROWS):
                    part = scores[j * MAX_ROWS : (j + 1) * MAX_ROWS]
                    peak = part if peak is None else jnp.maximum(peak, part)
            if 0 <= t - 1 < heads:
                p_buf[(t - 1) % 2, rows, :] = jnp.exp(
                    s_buf[(t - 1) % 2, rows, :] - peaks[t - 1]
                ).astype(BF)
            if 0 <= t - 2 < heads:
                part = matmul(vt[((t - 2) // 2) % 2, :, rows], p_buf[(t - 2) % 2, rows, :])
                total = part if total is None else total + part
        if t < heads:
            peaks[t] = jnp.max(peak, axis=0, keepdims=True)
            if not first:
                peaks[t] = jnp.maximum(peaks[t], stat_ref[t : t + 1, :])
        if 0 <= t - 2 < heads:
            head = t - 2
            side = head % 2
            own = slice(head * HDIM, (head + 1) * HDIM)
            norm = total[PAIR : PAIR + 1]
            mixed = total[side * HDIM : (side + 1) * HDIM]
            if first:
                o_ref[own, :] = mixed
                norms.append(norm)
                continue
            kept = jnp.exp(stat_ref[head : head + 1, :] - peaks[head])
            norm = norm + kept * stat_ref[8 + head : 9 + head, :]
            outs.append((mixed + kept * o_ref[own, :]) / norm)
            logs.append(peaks[head] + jnp.log(norm))
            if side == 1:
                pair = slice((head // 2) * PAIR, (head // 2 + 1) * PAIR)
                both = jnp.concatenate(outs[-2:], axis=0).T.astype(BF)
                mix0[:, pair] = both[:rows_q]
                mix1[:, pair] = both[rows_q:]
    spare = jnp.zeros((8 - heads, nq), F32)
    if first:
        stat_ref[...] = jnp.concatenate(
            [peaks[h] for h in range(heads)] + [spare] + norms + [spare], axis=0
        )
    else:
        for head in range(heads):
            lse_ref[head // 2, head % 2 : head % 2 + 1, :] = logs[head]


def near_kernel(core, *refs):
    xs, weights, masks = refs[:2], refs[2:9], refs[9:11]
    outs, tops, scratch = refs[11:19], refs[19:21], refs[21:]
    project_body(core, xs, weights, outs, True)
    for out in outs[:6]:
        out.send()
    a0, k0, v0, a1, k1, v1, q0, q1 = outs
    attend_body(True, (q0, q1), (k0, k1), (v0, v1), masks, None, tops, scratch)


def far_kernel(core, *refs):
    xs, weights, masks = refs[:2], refs[2:9], refs[9:11]
    queries, before, outs, tops, scratch = refs[11:13], refs[13:15], refs[15:21], refs[21:24], refs[24:]
    project_body(core, xs, weights, outs, False)
    for out in outs:
        out.send()
    a0, k0, v0, a1, k1, v1 = outs
    attend_body(False, queries, (k0, k1), (v0, v1), masks, before, tops, scratch)


def attend(core, xs, weights, masks, queries=(), before=()):
    rows, width = xs[0].shape
    half = width // 2
    heads = half // HDIM
    nq = nk = 2 * rows
    small = shape(BF, rows, half)
    outs = [shape(BF, rows, width), small, small] * 2
    if not before:
        outs += [small, small, shape(F32, half, nq), shape(F32, 16, nq)]
    else:
        outs += [small, small, shape(F32, heads // 2, 2, nq)]
    weight = by_core((width, half), 1)
    if not before:
        weights = [in_hbm(x) if x.ndim > 1 else x for x in weights]
    ins = (*xs, *weights, *masks, *queries, *before)
    return call(
        far_kernel if before else near_kernel,
        "attend",
        core,
        ins,
        [weight if x.shape == (width, width) else whole(*x.shape) for x in ins],
        outs,
        VMEM["far"] if before else VMEM["near"],
        [
            pltpu.VMEM((2, nk, nq), F32),
            pltpu.VMEM((2, nk, nq), BF),
            pltpu.VMEM((2, PAIR + SEGS, nq), BF),
            pltpu.VMEM((2, PAIR + 16, nk), BF),
            pltpu.VMEM((2, nk, PAIR + SEGS), BF),
        ],
        flops=2 * 2 * nq * nk * half * 4 + 2 * 2 * rows * width * half * 2,
        sent=tuple(range(6)) + ((8,) if before else ()),
    )


QUERY_BLOCK = 256


def attend_back_kernel(core, *refs):
    q0, q1, ks, vs = refs[0], refs[1], refs[2:6], refs[6:10]
    mq_ref, mk_ref, o0, o1, g0, g1, w_out, lse_ref, dq_ref, dk_ref, dv_ref, p_buf, ds_buf = refs[10:]
    nq = 2 * q0.shape[0]
    blocks = nq // QUERY_BLOCK
    nothing = jnp.zeros((), BF)
    upstream = jnp.concatenate([g0[...], g1[...]], axis=0)
    grad = trans_right(upstream, w_out[...]).astype(BF)
    query = jnp.concatenate([q0[...], q1[...]], axis=0)
    query_t, grad_t = query.T, grad.T
    key = jnp.concatenate([k[...] for k in ks], axis=0)
    value = jnp.concatenate([v[...] for v in vs], axis=0)
    key_t = key.T
    mixed = jnp.concatenate([o0[...], o1[...]], axis=0)
    product = grad_t.astype(F32) * mixed.T.astype(F32)
    key_masked = jnp.concatenate([key, mk_ref[...]], axis=1)
    mask_q = mq_ref[...]
    for b in range(blocks):
        cols = slice(b * QUERY_BLOCK, (b + 1) * QUERY_BLOCK)
        dqs = []
        for e in range(2):
            at = (e * blocks + b) * QUERY_BLOCK
            rows = head_rows(e, (PAIR, QUERY_BLOCK))
            query_e = jnp.where(rows, query_t[:, cols], nothing)
            grad_e = jnp.where(rows, grad_t[:, cols], nothing)
            scores = matmul(key_masked, jnp.concatenate([query_e, mask_q[:, cols]], axis=0))
            probs = jnp.exp(scores - lse_ref[0, e : e + 1, cols])
            p_buf[:, at : at + QUERY_BLOCK] = probs.astype(BF)
            grad_probs = matmul(value, grad_e)
            inner = jnp.sum(product[e * HDIM : (e + 1) * HDIM, cols], axis=0, keepdims=True)
            grad_scores = (probs * (grad_probs - inner)).astype(BF)
            ds_buf[:, at : at + QUERY_BLOCK] = grad_scores
            dqs.append(matmul(key_t, grad_scores)[e * HDIM : (e + 1) * HDIM])
        dq_ref[cols, :] = (jnp.concatenate(dqs, axis=0) * 0.125).T.astype(BF)

    def by_head(values):
        return jnp.concatenate(
            [jnp.where(head_lanes(e, values.shape), values, nothing) for e in range(2)], axis=0
        )

    dv_ref[...] = matmul(p_buf[...], by_head(grad)).astype(BF)
    dk_ref[...] = matmul(ds_buf[...], by_head(query)).astype(BF)


def attend_back(core, queries, keys, values, mask_q, mask_k, mixed, grads, w_out, lse):
    rows, width = queries[0].shape
    pairs = width // PAIR
    nq = 2 * rows
    nk = mask_k.shape[0]
    pair = lambda size: pl.BlockSpec((size, PAIR), lambda i, core: (0, i))
    outs = [shape(BF, size, width) for size in (nq, nk, nk)]
    ins = (*queries, *keys, *values, mask_q, mask_k, *mixed, *grads, w_out, lse)
    return pl.pallas_call(
        attend_back_kernel,
        grid_spec=pltpu.PrefetchScalarGridSpec(
            num_scalar_prefetch=1,
            grid=(pairs,),
            in_specs=[pair(rows)] * 10
            + [whole(SEGS, nq), whole(nk, SEGS)]
            + [pair(rows)] * 2
            + [whole(rows, 2 * width)] * 2
            + [pl.BlockSpec((PAIR, 2 * width), lambda i, core: (core[0] * pairs + i, 0))]
            + [pl.BlockSpec((1, 2, nq), lambda i, core: (i, 0, 0))],
            out_specs=[pair(nq), pair(nk), pair(nk)],
            scratch_shapes=[pltpu.VMEM((nk, 2 * nq), BF)] * 2,
        ),
        out_shape=outs,
        compiler_params=params(VMEM["attend_back"]),
        cost_estimate=pl.CostEstimate(
            flops=2 * 5 * nq * nk * width * 4,
            bytes_accessed=sum(x.size * x.dtype.itemsize for x in ins + tuple(outs)),
            transcendentals=0,
        ),
        name="attend_back",
    )(core, *ins)


def middle_kernel(core, x_ref, mine, other, w_out, b_out, gain, bias, h_ref, c_ref):
    half = mine.shape[1]
    at = pl.multiple_of(core[0] * half, 128)
    away = pl.multiple_of((1 - core[0]) * half, 128)
    hidden1 = x_ref[...].astype(F32) + (
        matmul(mine[...], w_out[pl.ds(at, half), :])
        + matmul(other[...], w_out[pl.ds(away, half), :])
        + b_out[...][None, :]
    )
    h_ref[...] = hidden1
    normed, _ = norm_forward(hidden1)
    c_ref[...] = (normed * gain[...][None, :] + bias[...][None, :]).astype(BF)


def middle(core, x, mine, other, w_out, b_out, gain, bias):
    rows, width = x.shape
    half = width // 2
    return call(
        middle_kernel,
        "middle",
        core,
        (x, mine, other, w_out, b_out, gain, bias),
        [whole(rows, width), whole(rows, half), whole(rows, half), whole(width, width)]
        + [whole(width)] * 3,
        [shape(F32, rows, width), shape(BF, rows, width)],
        VMEM["middle"],
        flops=2 * rows * width * width,
    )


HIDDEN_BLOCK = 512


def gelu_parts(values):
    bell = jnp.exp(values * values * -0.5)
    k = 1.0 / (1.0 + 0.23164188838 * jnp.abs(values))
    tail = 0.7107068705 + k * (-0.7265760135 + k * 0.5307027145)
    tail = k * (0.127414796 + k * (-0.142248368 + k * tail)) * bell
    below = jnp.where(values >= 0, 1.0 - tail, tail)
    return values * below, below + values * bell * 0.3989422804014327


def feed_kernel(core, c0, c1, g0, g1, w_up, b_up, w_down, act, gpre, db_up, dc0, dc1, pre, dact):
    rows = c0.shape[0]
    normed = jnp.concatenate([c0[...], c1[...]], axis=0)
    grad = jnp.concatenate([g0[...], g1[...]], axis=0)
    steps = w_up.shape[1] // HIDDEN_BLOCK
    bias = core_half(core, b_up)
    for t in range(steps + 1):
        if t < steps:
            part = slice(t * HIDDEN_BLOCK, (t + 1) * HIDDEN_BLOCK)
            pre[t % 2] = matmul(normed, w_up[:, part])
            dact[t % 2] = trans_right(grad, w_down[part, :])
        if t > 0:
            part = slice((t - 1) * HIDDEN_BLOCK, t * HIDDEN_BLOCK)
            value, slope = gelu_parts(pre[(t - 1) % 2] + bias[:, part])
            low = (dact[(t - 1) % 2] * slope).astype(BF)
            act[:, part] = value.astype(BF)
            gpre[:, part] = low
            db_up[:, part] = column_sum(low.astype(F32))
    grad_in = trans_right(gpre[...], w_up[...])
    dc0[...] = grad_in[:rows]
    dc1[...] = grad_in[rows:].astype(BF)


def feed(core, c0, c1, g0, g1, w_up, b_up, w_down):
    rows, width = c0.shape
    half = w_up.shape[1] // 2
    return call(
        feed_kernel,
        "feed",
        core,
        (c0, c1, g0, g1, w_up, b_up, w_down),
        [whole(rows, width)] * 4
        + [by_core((width, half), 1), whole(2 * half), by_core((half, width), 0)],
        [shape(BF, 2 * rows, half)] * 2
        + [shape(F32, 1, half), shape(F32, rows, width), shape(BF, rows, width)],
        VMEM["feed"],
        [pltpu.VMEM((2, 2 * rows, HIDDEN_BLOCK), F32)] * 2,
        pinned=(2,),
        flops=2 * 3 * 2 * rows * width * half,
    )


def feed_weights_kernel(core, c0, c1, g0, g1, act, gpre, dw_out, dw, sems):
    normed = jnp.concatenate([c0[...], c1[...]], axis=0)
    grad = jnp.concatenate([g0[...], g1[...]], axis=0)
    hidden = act.shape[1]
    copies = []
    for t in range(hidden // HIDDEN_BLOCK):
        part = slice(t * HIDDEN_BLOCK, (t + 1) * HIDDEN_BLOCK)
        turned = slice(hidden + t * HIDDEN_BLOCK, hidden + (t + 1) * HIDDEN_BLOCK)
        dw[part, :] = trans_left(act[:, part], grad).astype(BF)
        dw[turned, :] = trans_left(gpre[:, part], normed).astype(BF)
        for k, span in enumerate((part, turned)):
            copies.append(
                pltpu.make_async_copy(dw.at[span, :], dw_out.at[span, :], sems.at[2 * t + k])
            )
            copies[-1].start()
    for copy in copies:
        copy.wait()


def feed_weights(core, c0, c1, g0, g1, act, gpre):
    rows, width = c0.shape
    half = act.shape[1]
    ins = (c0, c1, g0, g1, act, gpre)
    return pl.pallas_call(
        feed_weights_kernel,
        grid_spec=pltpu.PrefetchScalarGridSpec(
            num_scalar_prefetch=1,
            grid=(1,),
            in_specs=[whole(*x.shape) for x in ins],
            out_specs=pl.BlockSpec(memory_space=pltpu.HBM),
            scratch_shapes=[
                pltpu.VMEM((2 * half, width), BF),
                pltpu.SemaphoreType.DMA((2 * half // HIDDEN_BLOCK,)),
            ],
        ),
        out_shape=pltpu.HBM((2 * half, width), BF),
        compiler_params=params(VMEM["feed_weights"]),
        cost_estimate=pl.CostEstimate(
            flops=2 * 2 * 2 * rows * width * half,
            bytes_accessed=2 * (4 * rows * width + 4 * rows * half + 2 * half * width),
            transcendentals=0,
        ),
        name="feed_weights",
    )(core, *ins)


def feed_out_kernel(core, act, w_down, out0, out1):
    rows = out0.shape[0]
    out = matmul(act[...], w_down[...])
    out0[...] = out[:rows]
    out1[...] = out[rows:].astype(BF)


def feed_out(core, act, w_down):
    rows, half = act.shape[0] // 2, act.shape[1]
    width = w_down.shape[1]
    return call(
        feed_out_kernel,
        "feed_out",
        core,
        (act, w_down),
        [whole(2 * rows, half), by_core((half, width), 0)],
        [shape(F32, rows, width), shape(BF, rows, width)],
        VMEM["feed_out"],
        flops=2 * 2 * rows * width * half,
    )


def middle_back_kernel(core, h_ref, own, got, g_ref, gain, out, low, sums):
    normed, rscale = norm_forward(h_ref[...])
    grad_in = own[...] + got[...].astype(F32)
    upstream = g_ref[...].astype(F32)
    grad = upstream + norm_back(grad_in * gain[...][None, :], normed, rscale)
    out[...] = grad
    rounded = grad.astype(BF)
    low[...] = rounded
    sums[...] = jnp.concatenate(
        [
            column_sum(grad_in * normed),
            column_sum(grad_in),
            column_sum(rounded.astype(F32)),
            column_sum(upstream),
            jnp.zeros((4, sums.shape[1]), F32),
        ],
        axis=0,
    )


def middle_back(core, hidden1, own, got, grad, gain):
    rows, width = hidden1.shape
    return call(
        middle_back_kernel,
        "middle_back",
        core,
        (hidden1, own, got, grad, gain),
        [whole(rows, width)] * 4 + [whole(width)],
        [shape(F32, rows, width), shape(BF, rows, width), shape(F32, 8, width)],
        VMEM["middle_back"],
        pinned=(0, 2),
    )


VECTORS = 16


def weights_back_kernel(core, *refs):
    attn, (dq, dk, dv, mix0, mix1, g0, g1, sums_2, db_up, grads) = refs[:4], refs[4:]
    rows, width = attn[0].shape
    half = width // 2
    a_near = jnp.concatenate([attn[0][...], attn[1][...]], axis=0)
    a_all = jnp.concatenate([a_near, attn[2][...], attn[3][...]], axis=0)
    mixed = jnp.concatenate([mix0[...], mix1[...]], axis=0)
    upstream = jnp.concatenate([g0[...], g1[...]], axis=0)
    stacked = [
        trans_left(dq[...], a_near),
        trans_left(dk[...], a_all),
        trans_left(dv[...], a_all),
        trans_left(mixed, upstream),
    ]
    share = half // 2
    for i, block in enumerate(stacked):
        low = block.astype(BF)
        grads[2 * i, :share, :] = low[:share]
        grads[2 * i + 1, :share, :] = low[share:]
    halves = jnp.concatenate(
        [column_sum(dq[...].astype(F32)), column_sum(dv[...].astype(F32))], axis=1
    )
    vectors = jnp.concatenate(
        [sums_2[0:4, :], db_up[:, :width], db_up[:, width:], halves]
        + [jnp.zeros((VECTORS - 7, width), F32)],
        axis=0,
    ).astype(BF)
    for i in range(8):
        grads[i, share:, :] = vectors


def weights_back(core, attn, dq, dk, dv, mixed, grads, sums_2, db_up):
    rows, width = attn[0].shape
    half = width // 2
    ins = (*attn, dq, dk, dv, *mixed, *grads, sums_2, db_up)
    return call(
        weights_back_kernel,
        "weights_back",
        core,
        ins,
        [whole(*x.shape) for x in ins],
        [shape(BF, 8, width // 4 + VECTORS, width)],
        VMEM["weights_back"],
        flops=2 * 6 * 2 * rows * width * half,
    )[0]


def terms_back_kernel(core, *refs):
    xs, (dq, dk, dv, wq, wk, wv, own, par, far, far_par, sums) = refs[:4], refs[4:]
    rows, width = xs[0].shape
    near = 2 * rows
    chip = trans_right(dk[:near], wk[...]) + trans_right(dv[:near], wv[...]) + trans_right(dq[...], wq[...])
    away = trans_right(dk[near:], wk[...]) + trans_right(dv[near:], wv[...])
    parts = (chip[:rows], chip[rows:], away[:rows], away[rows:])
    own[...] = parts[0]
    par[...] = parts[1].astype(BF)
    far[...] = parts[2]
    far_par[...] = parts[3].astype(BF)
    gain = jnp.zeros((1, width), F32)
    for x, terms in zip(xs, parts):
        normed, _ = norm_forward(x[...].astype(F32))
        gain = gain + column_sum(terms * normed)
    bias = column_sum(chip) + column_sum(away)
    sums[...] = jnp.concatenate([gain, bias, jnp.zeros((6, width), F32)], axis=0).astype(BF)


def terms_back(core, xs, dq, dk, dv, wq, wk, wv):
    rows, width = xs[0].shape
    half = width // 2
    weight = by_core((width, half), 1)
    ins = (*xs, dq, dk, dv, wq, wk, wv)
    return call(
        terms_back_kernel,
        "terms_back",
        core,
        ins,
        [weight if x.shape == (width, width) else whole(*x.shape) for x in ins],
        [shape(F32, rows, width), shape(BF, rows, width)] * 2 + [shape(BF, 8, width)],
        VMEM["terms_back"],
        flops=2 * 5 * 2 * rows * width * half,
    )


def finish_feed_kernel(core, mine_down, other_down, mine_up, other_up, w_down, w_up):
    ours = pl.program_id(0) == core[0]
    w_down[...] = jnp.where(ours, mine_down[0], other_down[0]).astype(F32)
    w_up[...] = jnp.where(ours, mine_up[0], other_up[0]).T.astype(F32)


def finish_feed(core, mine, other):
    _, block, width = mine.shape
    hidden = 8 * block

    def needed(half, first):
        def index(h, i, core):
            side = core[0] if half == 0 else 1 - core[0]
            at = jnp.where(h == side, i, jnp.where(h < side, 0, 3))
            return first + at, 0, 0

        return pl.BlockSpec((1, block, width), index)

    return pl.pallas_call(
        finish_feed_kernel,
        grid_spec=pltpu.PrefetchScalarGridSpec(
            num_scalar_prefetch=1,
            grid=(2, 4),
            in_specs=[needed(0, 0), needed(1, 0), needed(0, 4), needed(1, 4)],
            out_specs=[
                pl.BlockSpec((block, width), lambda h, i, core: (4 * h + i, 0)),
                pl.BlockSpec((width, block), lambda h, i, core: (0, 4 * h + i)),
            ],
        ),
        out_shape=[shape(F32, hidden, width), shape(F32, width, hidden)],
        compiler_params=params(VMEM["finish_feed"]),
        cost_estimate=pl.CostEstimate(flops=0, bytes_accessed=12 * hidden * width, transcendentals=0),
        name="finish_feed",
    )(core, mine, other, mine, other)


def finish_attend_kernel(core, mine, other, mine_vec, other_vec, wq, wk, wv, wo, *vecs):
    width = wq.shape[0]
    half = width // 2
    share = half // 2
    is_first = core[0] == 0
    for i, out in enumerate((wq, wk, wv, wo)):
        one, two = (
            jnp.concatenate([ref[2 * i, :share], ref[2 * i + 1, :share]], axis=0)
            for ref in (mine, other)
        )
        first = jnp.where(is_first, one, two)
        second = jnp.where(is_first, two, one)
        if i == 3:
            out[:half, :] = first.astype(F32)
            out[half:, :] = second.astype(F32)
        else:
            out[:, :half] = first.T.astype(F32)
            out[:, half:] = second.T.astype(F32)
    one, two = mine_vec[...].astype(F32), other_vec[...].astype(F32)
    both = one + two
    first = jnp.where(is_first, one, two)
    second = jnp.where(is_first, two, one)
    sums = sum(ref[i, share : share + 8].astype(F32) for ref in (mine, other) for i in range(8))
    for k in range(2):
        vecs[k][...] = sums[k]
    for k in range(4):
        vecs[2 + k][...] = both[k]
    up, query_bias, value_bias = vecs[6:]
    up[...] = jnp.concatenate([first[4], first[5], second[4], second[5]], axis=0)
    query_bias[...] = jnp.concatenate([first[6, :half], second[6, :half]], axis=0)
    value_bias[...] = jnp.concatenate([first[6, half:], second[6, half:]], axis=0)


def finish_attend(core, mine, other, mine_vec, other_vec, width, hidden):
    outs = [shape(F32, width, width)] * 4 + [shape(F32, width)] * 6
    outs += [shape(F32, hidden), shape(F32, width), shape(F32, width)]
    ins = (mine, other, mine_vec, other_vec)
    return call(
        finish_attend_kernel,
        "finish_attend",
        core,
        ins,
        [whole(*x.shape) for x in ins],
        outs,
        VMEM["finish_attend"],
    )


def finish_tokens_kernel(core, x, own, got, far, hidden_grad, gain, out):
    normed, rscale = norm_forward(x[...].astype(F32))
    grad = own[...] + got[...].astype(F32) + far[...].astype(F32)
    out[...] = hidden_grad[...] + norm_back(grad * gain[...][None, :], normed, rscale)


def finish_tokens(core, x, own, got, far, hidden_grad, gain):
    rows, width = x.shape
    return call(
        finish_tokens_kernel,
        "finish_tokens",
        core,
        (x, own, got, far, hidden_grad, gain),
        [whole(rows, width)] * 5 + [whole(width)],
        [shape(F32, rows, width)],
        VMEM["finish_tokens"],
    )[0]


def exchange(values, groups):
    return lax.all_to_all(values, BOTH, split_axis=0, concat_axis=0, axis_index_groups=groups)


def neighbours(axis):
    pairs = []
    for device in range(128):
        x, y, z, core = place_of(device)
        at = [x, y, z]
        at[axis] = 3 - at[axis] if core == 0 else at[axis] ^ 1
        x, y, z = at
        pairs.append((device, (x * 8 + (z // 2) * 4 + y) * 4 + (z % 2) * 2 + core))
    return pairs


ACROSS = [neighbours(axis) for axis in range(3)]


def add_along(parts, axes):
    got = [lax.ppermute(p, BOTH, ACROSS[axis]) for p, axis in zip(parts, axes)]
    return [(p.astype(F32) + g.astype(F32)).astype(BF) for p, g in zip(parts, got)]


def add_up_kernel(core, got, out):
    out[...] = sum(got[i].astype(F32) for i in range(8)).astype(BF)


def add_up(core, got):
    _, rows, width = got.shape
    return call(
        add_up_kernel, "add_up", core, (got,), [whole(*got.shape)], [shape(BF, rows, width)], VMEM["add_up"]
    )[0]


def per_device(
    tokens,
    lengths,
    ln1_gain,
    ln1_bias,
    w_query,
    b_query,
    w_key,
    w_value,
    b_value,
    w_out,
    b_out,
    ln2_gain,
    ln2_bias,
    w_up,
    b_up,
    w_down,
    b_down,
    cotangent,
):
    _, rows, width = tokens.shape
    hidden = w_up.shape[1]
    band = lax.axis_index("band")
    core = lax.rem(band, 2).reshape(1)
    together = lax.optimization_barrier

    own = tokens.reshape(rows, width)
    grad_own = cotangent.reshape(rows, width)
    far = swap_z(own)
    par = swap_core(own)
    grad_par = swap_core(grad_own)

    ends = jnp.cumsum(lengths[0])
    place = jnp.arange(rows, dtype=jnp.int32)
    slices = [band, band ^ 1, band ^ 2, band ^ 3]
    at_all = jnp.concatenate([s * rows + place for s in slices])
    seg_all = jnp.sum((at_all[:, None] >= ends[None, :]).astype(jnp.int32), axis=1)
    lanes = jnp.arange(SEGS, dtype=jnp.int32)
    count = lengths.shape[1]
    mask_q = (seg_all[None, : 2 * rows] == lanes[:, None]).astype(BF)
    mask_k = jnp.where(
        (seg_all[:, None] != lanes[None, :]) & (lanes[None, :] < count), -BARRED, 0.0
    ).astype(BF)

    params = (ln1_gain, ln1_bias, w_query, b_query, w_key, w_value, b_value)
    *near, q0, q1, part, stats = attend(core, (own, par), params, (mask_q, mask_k[: 2 * rows]))
    queries, before = (q0, q1), (part, stats)
    far, before, grad_par = together((far, before, grad_par))
    far_par = swap_core(far)
    *away, mix_own, mix_par, lse = attend(
        core, (far, far_par), params, (mask_q, mask_k[2 * rows :]), queries, before
    )
    attn, keys, values = ((near[i], near[3 + i], away[i], away[3 + i]) for i in range(3))
    mix_other = swap_core(mix_par)
    hidden1, mlp_own = middle(core, own, mix_own, mix_other, w_out, b_out, ln2_gain, ln2_bias)
    mlp_par = swap_core(mlp_own)
    sides = (mlp_own, mlp_par, grad_own, grad_par)
    act, gpre, db_up, dc_own, dc_par = feed(core, *sides, w_up, b_up, w_down)
    dc_got = swap_core(dc_par)
    group_1 = feed_weights(core, *sides, act, gpre)
    dc_got, group_1 = together((dc_got, group_1))
    dc_got = in_hbm(dc_got)
    grad_hidden1, grad_attn, sums_2 = middle_back(core, hidden1, dc_own, dc_got, grad_own, ln2_gain)
    grads = (grad_attn, swap_core(grad_attn))
    grads, group_1 = together((grads, group_1))
    mixed = (mix_own, mix_par)
    got_1 = exchange(group_1.reshape(8, -1, width), GROUPS_1)
    dq, dk, dv = attend_back(
        core, queries, keys, values, mask_q, mask_k, mixed, grads, w_out, lse
    )
    group_2 = weights_back(core, attn, dq, dk, dv, mixed, grads, sums_2, db_up)
    got_1, group_2 = together((got_1, group_2))
    got_2 = exchange(group_2, GROUPS_1)
    part_1 = add_up(core, got_1)
    part_1, dq = together((part_1, dq))
    (part_1,) = add_along([part_1], (0,))
    t_own, t_par, t_far, t_far_par, sums_1 = terms_back(
        core, (own, par, far, far_par), dq, dk, dv, w_query, w_key, w_value
    )
    part_1, t_par, t_far_par = together((part_1, t_par, t_far_par))
    (part_1,) = add_along([part_1], (1,))
    got_far, got_own = swap_core(t_far_par), swap_core(t_par)
    far_sum = (t_far + got_far.astype(F32)).astype(BF)
    part_1, got_2, far_sum, got_own = together((part_1, got_2, far_sum, got_own))
    part_2 = add_up(core, got_2)
    share = width // 4
    rest = jnp.concatenate([part_2[: share + VECTORS - 2], sums_1[:2]], axis=0)
    far_terms = swap_z(far_sum)
    part_1, rest = add_along([part_1, rest], (2, 0))
    part_1, rest = together((part_1, rest))

    def spread(values):
        return exchange(jnp.broadcast_to(values[None], (8,) + values.shape), GROUPS_1)

    total_1 = spread(part_1)
    (rest,) = add_along([rest], (1,))
    (rest,) = add_along([rest], (2,))
    act, _ = together((act, part_1))
    out_own, out_par = feed_out(core, act, w_down)
    layer_out = (hidden1 + out_own + swap_core(out_par).astype(F32) + b_down).astype(BF)
    total_1, rest, layer_out = together((total_1, rest, layer_out))
    vectors = rest[share:]
    total_2 = spread(jnp.concatenate([rest[:share], vectors[-2:], vectors[:6]], axis=0))
    total_1, far_terms = together((total_1, far_terms))
    other_1 = swap_core(total_1)
    other_vectors = swap_core(vectors)
    full_down, full_up = finish_feed(core, total_1, other_1)
    total_2, full_down, other_vectors, t_own = together(
        (total_2, full_down, other_vectors, t_own)
    )
    other_2 = swap_core(total_2)
    grad_tokens = finish_tokens(core, own, t_own, got_own, far_terms, grad_hidden1, ln1_gain)
    other_2, grad_tokens = together((other_2, grad_tokens))
    finished = finish_attend(core, total_2, other_2, vectors, other_vectors, width, hidden)
    full_query, full_key, full_value, full_out = finished[:4]
    d_gain1, d_bias1, d_gain2, d_bias2, d_b_out, d_b_down, d_b_up, d_b_query, d_b_value = finished[4:]
    return (
        layer_out[None],
        grad_tokens[None],
        d_gain1,
        d_bias1,
        full_query,
        d_b_query,
        full_key,
        full_value,
        d_b_value,
        full_out,
        d_b_out,
        d_gain2,
        d_bias2,
        full_up,
        d_b_up,
        full_down,
        d_b_down,
    )


def solution(mesh):
    split = P("dp", "band", None)
    return jax.shard_map(
        per_device,
        mesh=mesh,
        in_specs=(split, P("dp", None)) + (P(),) * 15 + (split,),
        out_specs=(split, split) + (P(),) * 15,
        check_vma=False,
    )
```
